128 devices in a mesh: req: 8 (over x, core), score: 16 (over z, y).
Axes of the slice: x: 4, y: 4, z: 4, core: 2. Of those that a mesh axis runs over, the one named last changes fastest.
Arguments:
- cand_ids: int32 [32, 2048], P('req', 'score'), may hold values from 0 to 131071, as said below
- table_slab: bfloat16 [131072, 1024], P(('req', 'score')), may hold values from -6 to 6
- user_rows: bfloat16 [32, 1024], P('req', 'score'), may hold values from -6 to 6
- cross_weight: bfloat16 [2, 2048, 2048], replicated, may hold values from -0.125 to 0.125
- cross_bias: float32 [2, 2048], replicated, may hold values from -3 to 3
- hidden_weight: bfloat16 [2048, 1024], replicated, may hold values from -0.125 to 0.125
- hidden_bias: float32 [1024], replicated, may hold values from -3 to 3
- out_weight: bfloat16 [1024], replicated, may hold values from -0.1875 to 0.1875
Outputs:
- scores: float32 [32, 2048], P('req', 'score')
The draws below stay inside these ranges and needn't reach their ends.
Inputs may be any that keep to these rules, and one draw needn't show every extreme that they name: `cand_ids`: table rows d * 1024 to (d + 1) * 1024 - 1 lie on device d of req+score. Of the candidates of one device, at most 8 lie on the rows of any one device, and some device's rows hold exactly 8 candidates of every device. Ids may repeat.
All inputs are finite; a program needn't handle non-finite values.
Results may differ from the reference program's by a relative error of at most 0.0039.
Values may be sent and summed in bfloat16 or wider, within the bound.
No kernel may reach another device: no remote copies, remote signals or barrier semaphores. Data moves between devices by JAX's collectives and lax.ppermute only.
A program may use at most 128 MiB of HBM per device.

```python
import jax
import jax.numpy as jnp
from jax import lax

UW = 1024
IW = 1024
CROSS = 2048
HID = 1024
LAYERS = 2
REQ_G = 4
CAND = 2048
ROWS_DEV = 1024
REQS = 32
TABLE_ROWS = 131072
CAP = 8
N_REQ = 8
N_SCORE = 16


def draw_cand_ids(key, part):
    key = jax.random.fold_in(key, 11)
    devices = N_REQ * N_SCORE
    per_device = REQ_G * CAND // N_SCORE
    slots = devices * CAP
    favor_key, bias_key, rest_key = jax.random.split(key, 3)
    favored = jax.random.randint(favor_key, (), 0, devices)
    owner_bias = jax.random.randint(bias_key, (devices,), 0, 3)
    owner_of_slot = jnp.arange(slots, dtype=jnp.int32) // CAP

    def one_device(sub):
        order_key, local_key, shuffle_key = jax.random.split(sub, 3)
        order = jax.random.permutation(order_key, slots).astype(jnp.int32)
        priority = order + owner_bias[owner_of_slot] * (slots // 2)
        priority = jnp.where(owner_of_slot == favored, -1, priority)
        picked = jnp.argsort(priority, stable=True)[:per_device]
        picked = picked[jax.random.permutation(shuffle_key, per_device)]
        owners = (picked // CAP).astype(jnp.int32)
        local_rows = jax.random.randint(local_key, (per_device,), 0, ROWS_DEV)
        return owners * ROWS_DEV + local_rows
    blocks = jax.vmap(one_device)(jax.random.split(rest_key, devices))
    blocks = blocks.reshape(N_REQ, N_SCORE, REQ_G, CAND // N_SCORE)
    blocks = jnp.transpose(blocks, (0, 2, 1, 3))
    return blocks.reshape(REQ_G * N_REQ, CAND).astype(jnp.int32)


def levels(stream_key, shape, pieces, smallest, top_value):
    def one(axis_at, shards_of):
        steps = jax.random.uniform(jax.random.fold_in(jax.random.fold_in(stream_key, 6), axis_at), (shards_of,), jnp.float32, smallest / len(pieces), top_value / len(pieces))
        return jnp.repeat(jnp.exp(steps), shape[axis_at] // shards_of).reshape((-1,) + (1,) * (len(shape) - axis_at - 1))

    level = one(*pieces[0])
    for cut in pieces[1:]:
        level = level * one(*cut)
    return level


def gaussian(key, shape, width, most, cuts=(), kind=jnp.bfloat16):
    drawn = jax.random.normal(key, shape, jnp.float32) * width
    if len(cuts) > 0:
        drawn = levels(key, shape, cuts, -0.22, 0.18) * drawn
    return jnp.clip(drawn, min=-most, max=most).astype(kind)


def setup_inputs(seed: int = 0) -> dict:
    seeds = jax.random.split(jax.random.key(seed), 9)
    return {
        "cand_ids": draw_cand_ids(jax.random.fold_in(seeds[8], 71), 0),
        "table_slab": gaussian(seeds[1], (TABLE_ROWS, IW), 1.0, 6.0, ((0, 128),)),
        "user_rows": gaussian(seeds[2], (REQS, UW), 1.0, 6.0, ((0, 8), (1, 16))),
        "cross_weight": gaussian(seeds[3], (LAYERS, CROSS, CROSS), CROSS ** -0.5, 0.125),
        "cross_bias": gaussian(seeds[4], (LAYERS, CROSS), 0.5, 3.0, (), jnp.float32),
        "hidden_weight": gaussian(seeds[5], (CROSS, HID), CROSS ** -0.5, 0.125),
        "hidden_bias": gaussian(seeds[6], (HID,), 0.5, 3.0, (), jnp.float32),
        "out_weight": gaussian(seeds[7], (HID,), HID ** -0.5, 0.1875),
    }


def score_request(args, table_slab, cross_weight, cross_bias, hidden_weight, hidden_bias, out_weight):
    id_list, user_vector = args
    items = table_slab[id_list]
    user_rep = jnp.broadcast_to(user_vector[None, :], (id_list.shape[0], user_vector.shape[0]))
    first = jnp.concatenate([user_rep, items], axis=1)
    first_float = first.astype(jnp.float32)
    state = first_float
    for layer_index in range(LAYERS):
        mixed = jnp.dot(state.astype(jnp.bfloat16), cross_weight[layer_index], preferred_element_type=jnp.float32)
        state = first_float * (mixed + cross_bias[layer_index]) + state
    hidden = jnp.dot(state.astype(jnp.bfloat16), hidden_weight, preferred_element_type=jnp.float32)
    hidden = jax.nn.relu(hidden + hidden_bias).astype(jnp.bfloat16)
    logit = jnp.dot(hidden, out_weight, preferred_element_type=jnp.float32)
    return jax.nn.sigmoid(logit)


def reference(cand_ids, table_slab, user_rows, cross_weight, cross_bias, hidden_weight, hidden_bias, out_weight):
    def worker(args):
        return score_request(args, table_slab, cross_weight, cross_bias, hidden_weight, hidden_bias, out_weight)
    return lax.map(worker, (cand_ids, user_rows))
```

```python
import jax
import jax.numpy as jnp
from jax import lax
from jax.experimental import pallas as pl
from jax.experimental.pallas import tpu as pltpu
from jax.sharding import PartitionSpec as P

BF = jnp.bfloat16
F32 = jnp.float32
AXES = ("req", "score")
CAP = 8
LANES = 128
WORDS = 4


def iota(shape, axis):
    return lax.broadcasted_iota(jnp.int32, shape, axis)


def prepare_kernel(ids_ref, user_ref, msg_ref, key_ref):
    groups, width = ids_ref.shape
    devices = msg_ref.shape[0] // WORDS
    ids = ids_ref[...]
    owner = ids >> 10
    local = ids & 1023
    upto = (iota((width, width), 0) <= iota((width, width), 1)).astype(BF)
    device_row = iota((devices, width), 0)
    base = jnp.zeros((devices, 1), F32)
    high = jnp.zeros((devices, LANES), F32)
    low = jnp.zeros((devices, LANES), F32)
    contract_last = (((1,), (1,)), ((), ()))
    for q in range(groups):
        mine = device_row == owner[q : q + 1, :]
        onehot = mine.astype(BF)
        count = jnp.dot(onehot, upto, preferred_element_type=F32) + base
        rank = jnp.sum(jnp.where(mine, count, 0.0), axis=0, keepdims=True) - 1.0
        rank = rank.astype(jnp.int32)
        base = count[:, width - 1 : width]
        value = local[q : q + 1, :] * groups + (q + 1)
        at_rank = iota((LANES, width), 0) == rank
        value_high = jnp.where(at_rank, value >> 4, 0).astype(F32).astype(BF)
        value_low = jnp.where(at_rank, value & 15, 0).astype(F32).astype(BF)
        high += lax.dot_general(onehot, value_high, contract_last, preferred_element_type=F32)
        low += lax.dot_general(onehot, value_low, contract_last, preferred_element_type=F32)
        key_ref[q : q + 1, :] = owner[q : q + 1, :] * CAP + rank
    user = user_ref[...].astype(F32)
    pairs = [
        jnp.concatenate([user[2 * p : 2 * p + 1, :], user[2 * p + 1 : 2 * p + 2, :]], axis=1)
        for p in range(2)
    ]
    msg_ref[pl.ds(0, devices, stride=WORDS), :] = high * 16.0 + low
    for p in range(2):
        msg_ref[pl.ds(p + 1, devices, stride=WORDS), :] = jnp.broadcast_to(
            pairs[p], (devices, LANES)
        )
    msg_ref[pl.ds(3, devices, stride=WORDS), :] = jnp.zeros((devices, LANES), F32)


def score_kernel(
    msg_ref,
    slab_ref,
    cross_ref,
    cross_bias_ref,
    hidden_ref,
    hidden_bias_ref,
    out_ref,
    score_ref,
    users,
    shift,
    items_hot,
    users_hot,
    first,
    state,
    state_bf,
    logits,
):
    devices = msg_ref.shape[0] // WORDS
    rows = slab_ref.shape[0]
    item_width = slab_ref.shape[1]
    cross = cross_ref.shape[1]
    user_width = cross - item_width
    hid = hidden_ref.shape[1]
    slots = CAP * devices
    per_req = devices // 8
    left = iota((8, LANES), 1) < 64
    for t in range(user_width // LANES):
        for p in range(2):
            even = msg_ref[pl.ds(8 * t + 1 + p, 8, stride=WORDS * per_req), :]
            odd = msg_ref[pl.ds(8 * t + 5 + p, 8, stride=WORDS * per_req), :]
            cols = slice(t * LANES, (t + 1) * LANES)
            users[16 * p : 16 * p + 8, cols] = jnp.where(left, even, pltpu.roll(odd, 64, 1))
            users[16 * p + 8 : 16 * p + 16, cols] = jnp.where(left, pltpu.roll(even, 64, 1), odd)
    users_bf = users[...].astype(BF)
    value = msg_ref[pl.ds(0, devices, stride=WORDS), :].astype(jnp.int32) - 1
    row_of = value >> 2
    req_of = (value & 3) * 8 + iota((devices, LANES), 0) // per_req
    row_lane = iota((devices, rows), 1)
    req_lane = iota((devices, LANES), 1)
    for k in range(CAP):
        part = slice(k * devices, (k + 1) * devices)
        items_hot[part, :] = (row_lane == row_of[:, k : k + 1]).astype(BF)
        users_hot[part, :] = ((req_lane & 31) == req_of[:, k : k + 1]).astype(BF)
    base = jnp.dot(users_bf, cross_ref[0, :user_width, :], preferred_element_type=F32)
    base = base + (cross_bias_ref[0:1, :] + 1.0)
    base_high = base.astype(BF)
    rest = base - base_high.astype(F32)
    base_mid = rest.astype(BF)
    base_low = (rest - base_mid.astype(F32)).astype(BF)
    shift[0:32, :] = base_high
    shift[32:64, :] = base_mid
    shift[64:96, :] = base_low
    shift[96:128, :] = jnp.zeros_like(base_low)
    first[:, :user_width] = jnp.dot(
        users_hot[:, :32], users_bf, preferred_element_type=F32
    ).astype(BF)
    first[:, user_width:] = jnp.dot(
        items_hot[...], slab_ref[...], preferred_element_type=F32
    ).astype(BF)
    tile = 1024

    def layer_one(n, carry):
        cols = pl.ds(pl.multiple_of(n * tile, tile), tile)
        factor = jnp.dot(
            first[:, user_width:], cross_ref[0, user_width:, cols], preferred_element_type=F32
        )
        factor += jnp.dot(users_hot[...], shift[:, cols], preferred_element_type=F32)
        new = first[:, cols].astype(F32) * factor
        state[:, cols] = new
        state_bf[:, cols] = new.astype(BF)
        return carry

    lax.fori_loop(0, cross // tile, layer_one, 0)

    def layer_two(n, carry):
        cols = pl.ds(pl.multiple_of(n * tile, tile), tile)
        mixed = jnp.dot(state_bf[...], cross_ref[1, :, cols], preferred_element_type=F32)
        mixed += cross_bias_ref[1:2, cols]
        state[:, cols] = first[:, cols].astype(F32) * mixed + state[:, cols]
        return carry

    lax.fori_loop(0, cross // tile, layer_two, 0)
    state_bf[...] = state[...].astype(BF)
    hidden = jnp.dot(state_bf[...], hidden_ref[...], preferred_element_type=F32)
    hidden = jnp.maximum(hidden + hidden_bias_ref[...], 0.0).astype(BF)
    logits[...] = jnp.dot(hidden, out_ref[...], preferred_element_type=F32)
    lane = iota((devices, LANES), 1)
    total = jnp.zeros((devices, LANES), F32)
    for k in range(CAP):
        total = jnp.where(lane == k, logits[k * devices : (k + 1) * devices, :], total)
    score_ref[...] = jax.nn.sigmoid(total)


def collect_kernel(scores_ref, key_ref, out_ref):
    groups, width = key_ref.shape
    devices = scores_ref.shape[0]
    scores = scores_ref[...]
    for q in range(groups):
        key = key_ref[q : q + 1, :]
        total = jnp.zeros((devices, width), F32)
        for k in range(CAP):
            here = iota((devices, width), 0) * CAP + k == key
            total += jnp.where(here, scores[:, k : k + 1], 0.0)
        out_ref[q : q + 1, :] = jnp.sum(total, axis=0, keepdims=True)


def per_device(
    cand_ids,
    table_slab,
    user_rows,
    cross_weight,
    cross_bias,
    hidden_weight,
    hidden_bias,
    out_weight,
):
    devices = lax.axis_size("req") * lax.axis_size("score")
    groups, width = cand_ids.shape
    slots = devices * CAP
    cross = cross_weight.shape[1]
    hid = hidden_weight.shape[1]
    vmem = pl.BlockSpec(memory_space=pltpu.VMEM)
    msg, key = pl.pallas_call(
        prepare_kernel,
        out_shape=(
            jax.ShapeDtypeStruct((devices * WORDS, LANES), F32),
            jax.ShapeDtypeStruct((groups, width), jnp.int32),
        ),
        in_specs=[vmem, vmem],
        out_specs=(vmem, vmem),
        name="prepare",
    )(cand_ids, user_rows)
    asked = lax.all_to_all(msg, AXES, split_axis=0, concat_axis=0, tiled=True)
    out_columns = jnp.broadcast_to(out_weight[:, None], (hid, LANES))
    scores = pl.pallas_call(
        score_kernel,
        out_shape=jax.ShapeDtypeStruct((devices, LANES), F32),
        in_specs=[vmem] * 7,
        out_specs=vmem,
        scratch_shapes=[
            pltpu.VMEM((32, cross // 2), F32),
            pltpu.VMEM((LANES, cross), BF),
            pltpu.VMEM((slots, table_slab.shape[0]), BF),
            pltpu.VMEM((slots, LANES), BF),
            pltpu.VMEM((slots, cross), BF),
            pltpu.VMEM((slots, cross), F32),
            pltpu.VMEM((slots, cross), BF),
            pltpu.VMEM((slots, LANES), F32),
        ],
        compiler_params=pltpu.CompilerParams(vmem_limit_bytes=58 * 2**20),
        name="score",
    )(
        asked,
        table_slab,
        cross_weight,
        cross_bias,
        hidden_weight,
        hidden_bias.reshape(1, hid),
        out_columns,
    )
    answered = lax.all_to_all(scores, AXES, split_axis=0, concat_axis=0, tiled=True)
    return pl.pallas_call(
        collect_kernel,
        out_shape=jax.ShapeDtypeStruct((groups, width), F32),
        in_specs=[vmem, vmem],
        out_specs=vmem,
        name="collect",
    )(answered, key)


def solution(mesh):
    placed = (
        P("req", "score"),
        P(("req", "score"), None),
        P("req", "score"),
        P(),
        P(),
        P(),
        P(),
        P(),
    )
    return jax.shard_map(
        per_device, mesh=mesh, in_specs=placed, out_specs=P("req", "score"), check_vma=False
    )
```

```python
import jax
import jax.numpy as jnp
from jax import lax
from jax.experimental import pallas as pl
from jax.experimental.pallas import tpu as pltpu
from jax.sharding import PartitionSpec as P

BF = jnp.bfloat16
F32 = jnp.float32
AXES = ("req", "score")
CAP = 8
LANES = 128
WORDS = 4


def iota(shape, axis):
    return lax.broadcasted_iota(jnp.int32, shape, axis)


def prepare_kernel(ids_ref, user_ref, msg_ref, key_ref):
    groups, width = ids_ref.shape
    devices = msg_ref.shape[0] // WORDS
    ids = ids_ref[...]
    owner = ids >> 10
    local = ids & 1023
    upto = (iota((width, width), 0) <= iota((width, width), 1)).astype(BF)
    device_row = iota((devices, width), 0)
    base = jnp.zeros((devices, 1), F32)
    high = jnp.zeros((devices, LANES), F32)
    low = jnp.zeros((devices, LANES), F32)
    contract_last = (((1,), (1,)), ((), ()))
    for q in range(groups):
        mine = device_row == owner[q : q + 1, :]
        onehot = mine.astype(BF)
        count = jnp.dot(onehot, upto, preferred_element_type=F32) + base
        rank = jnp.sum(jnp.where(mine, count, 0.0), axis=0, keepdims=True) - 1.0
        rank = rank.astype(jnp.int32)
        base = count[:, width - 1 : width]
        value = local[q : q + 1, :] * groups + (q + 1)
        at_rank = iota((LANES, width), 0) == rank
        value_high = jnp.where(at_rank, value >> 4, 0).astype(F32).astype(BF)
        value_low = jnp.where(at_rank, value & 15, 0).astype(F32).astype(BF)
        high += lax.dot_general(onehot, value_high, contract_last, preferred_element_type=F32)
        low += lax.dot_general(onehot, value_low, contract_last, preferred_element_type=F32)
        key_ref[q : q + 1, :] = owner[q : q + 1, :] * CAP + rank
    user = user_ref[...].astype(F32)
    pairs = [
        jnp.concatenate([user[2 * p : 2 * p + 1, :], user[2 * p + 1 : 2 * p + 2, :]], axis=1)
        for p in range(2)
    ]
    msg_ref[pl.ds(0, devices, stride=WORDS), :] = high * 16.0 + low
    for p in range(2):
        msg_ref[pl.ds(p + 1, devices, stride=WORDS), :] = jnp.broadcast_to(
            pairs[p], (devices, LANES)
        )
    msg_ref[pl.ds(3, devices, stride=WORDS), :] = jnp.zeros((devices, LANES), F32)


def score_kernel(
    msg_ref,
    slab_hbm,
    cross_hbm,
    cross_bias_ref,
    hidden_hbm,
    hidden_bias_ref,
    out_ref,
    score_ref,
    slab_ref,
    cross_ref,
    hidden_ref,
    copied,
    users,
    shift,
    items_hot,
    users_hot,
    first,
    state,
    state_one,
    state_two,
    hidden,
):
    devices = msg_ref.shape[0] // WORDS
    rows = slab_ref.shape[0]
    item_width = slab_ref.shape[1]
    cross = cross_ref.shape[1]
    user_width = cross - item_width
    hid = hidden_ref.shape[1]
    slots = CAP * devices
    per_req = devices // 8
    half = 512
    tile = 512
    parts = [slice(h, h + half) for h in range(0, slots, half)]

    def tiles(width):
        return [slice(n, n + tile) for n in range(0, width, tile)]

    lower, upper = pl.ds(0, user_width), pl.ds(user_width, item_width)
    copies = [
        pltpu.make_async_copy(source, target, copied.at[i])
        for i, (source, target) in enumerate(
            [
                (slab_hbm, slab_ref),
                (cross_hbm.at[0, lower], cross_ref.at[0, lower]),
                (cross_hbm.at[0, upper], cross_ref.at[0, upper]),
                (cross_hbm.at[1], cross_ref.at[1]),
                (hidden_hbm, hidden_ref),
            ]
        )
    ]
    for copy in copies:
        copy.start()
    slab_here, cross_user_here, cross_item_here, cross_two_here, hidden_here = copies
    left = iota((8, LANES), 1) < 64
    for t in range(user_width // LANES):
        for p in range(2):
            even = msg_ref[pl.ds(8 * t + 1 + p, 8, stride=WORDS * per_req), :]
            odd = msg_ref[pl.ds(8 * t + 5 + p, 8, stride=WORDS * per_req), :]
            cols = slice(t * LANES, (t + 1) * LANES)
            users[16 * p : 16 * p + 8, cols] = jnp.where(left, even, pltpu.roll(odd, 64, 1))
            users[16 * p + 8 : 16 * p + 16, cols] = jnp.where(left, pltpu.roll(even, 64, 1), odd)
    users_bf = users[...].astype(BF)
    value = msg_ref[pl.ds(0, devices, stride=WORDS), :].astype(jnp.int32) - 1
    row_of = value >> 2
    req_of = (value & 3) * 8 + iota((devices, LANES), 0) // per_req
    row_lane = iota((devices, rows), 1)
    req_lane = iota((devices, LANES), 1)
    for k in range(CAP):
        part = slice(k * devices, (k + 1) * devices)
        items_hot[part, :] = (row_lane == row_of[:, k : k + 1]).astype(BF)
        users_hot[part, :] = ((req_lane & 31) == req_of[:, k : k + 1]).astype(BF)
    slab_here.wait()
    for part in parts:
        for cols in tiles(item_width):
            first[part, user_width + cols.start : user_width + cols.stop] = jnp.dot(
                items_hot[part, :], slab_ref[:, cols], preferred_element_type=F32
            ).astype(BF)
    cross_user_here.wait()
    base = jnp.dot(users_bf, cross_ref[0, :user_width, :], preferred_element_type=F32)
    base = base + (cross_bias_ref[0:1, :] + 1.0)
    base_high = base.astype(BF)
    rest = base - base_high.astype(F32)
    base_mid = rest.astype(BF)
    base_low = (rest - base_mid.astype(F32)).astype(BF)
    shift[0:32, :] = base_high
    shift[32:64, :] = base_mid
    shift[64:96, :] = base_low
    shift[96:128, :] = jnp.zeros_like(base_low)
    for part in parts:
        for cols in tiles(user_width):
            first[part, cols] = jnp.dot(
                users_hot[part, :32], users_bf[:, cols], preferred_element_type=F32
            ).astype(BF)
    cross_item_here.wait()
    for part in parts:
        for cols in tiles(cross):
            factor = jnp.dot(
                first[part, user_width:],
                cross_ref[0, user_width:, cols],
                preferred_element_type=F32,
            )
            factor += jnp.dot(users_hot[part, :], shift[:, cols], preferred_element_type=F32)
            new = first[part, cols].astype(F32) * factor
            state[part, cols] = new
            state_one[part, cols] = new.astype(BF)
    cross_two_here.wait()
    for part in parts:
        for cols in tiles(cross):
            mixed = jnp.dot(
                state_one[part, :], cross_ref[1, :, cols], preferred_element_type=F32
            )
            mixed += cross_bias_ref[1:2, cols]
            new = first[part, cols].astype(F32) * mixed + state[part, cols]
            state_two[part, cols] = new.astype(BF)
    hidden_here.wait()
    for part in parts:
        for cols in tiles(hid):
            got = jnp.dot(state_two[part, :], hidden_ref[:, cols], preferred_element_type=F32)
            hidden[part, cols] = jnp.maximum(got + hidden_bias_ref[:, cols], 0.0).astype(BF)
    out_rows = jnp.broadcast_to(out_ref[...], (LANES, hid))
    lane = iota((devices, LANES), 1)
    total = jnp.zeros((devices, LANES), F32)
    for part in parts:
        logits = lax.dot_general(
            hidden[part, :], out_rows, (((1,), (1,)), ((), ())), preferred_element_type=F32
        )
        for k in range(half // devices):
            here = lane == part.start // devices + k
            total = jnp.where(here, logits[k * devices : (k + 1) * devices, :], total)
    score_ref[...] = jax.nn.sigmoid(total)


def collect_kernel(scores_ref, key_ref, out_ref):
    groups, width = key_ref.shape
    devices = scores_ref.shape[0]
    scores = scores_ref[...]
    for q in range(groups):
        key = key_ref[q : q + 1, :]
        total = jnp.zeros((devices, width), F32)
        for k in range(CAP):
            here = iota((devices, width), 0) * CAP + k == key
            total += jnp.where(here, scores[:, k : k + 1], 0.0)
        out_ref[q : q + 1, :] = jnp.sum(total, axis=0, keepdims=True)


def per_device(
    cand_ids,
    table_slab,
    user_rows,
    cross_weight,
    cross_bias,
    hidden_weight,
    hidden_bias,
    out_weight,
):
    devices = lax.axis_size("req") * lax.axis_size("score")
    groups, width = cand_ids.shape
    slots = devices * CAP
    cross = cross_weight.shape[1]
    hid = hidden_weight.shape[1]
    vmem = pl.BlockSpec(memory_space=pltpu.VMEM)
    hbm = pl.BlockSpec(memory_space=pl.ANY)
    msg, key = pl.pallas_call(
        prepare_kernel,
        out_shape=(
            jax.ShapeDtypeStruct((devices * WORDS, LANES), F32),
            jax.ShapeDtypeStruct((groups, width), jnp.int32),
        ),
        in_specs=[vmem, vmem],
        out_specs=(vmem, vmem),
        name="prepare",
    )(cand_ids, user_rows)
    asked = lax.all_to_all(msg, AXES, split_axis=0, concat_axis=0, tiled=True)
    scores = pl.pallas_call(
        score_kernel,
        out_shape=jax.ShapeDtypeStruct((devices, LANES), F32),
        in_specs=[vmem, hbm, hbm, vmem, hbm, vmem, vmem],
        out_specs=vmem,
        scratch_shapes=[
            pltpu.VMEM(table_slab.shape, BF),
            pltpu.VMEM(cross_weight.shape, BF),
            pltpu.VMEM(hidden_weight.shape, BF),
            pltpu.SemaphoreType.DMA((5,)),
            pltpu.VMEM((32, cross // 2), F32),
            pltpu.VMEM((LANES, cross), BF),
            pltpu.VMEM((slots, table_slab.shape[0]), BF),
            pltpu.VMEM((slots, LANES), BF),
            pltpu.VMEM((slots, cross), BF),
            pltpu.VMEM((slots, cross), F32),
            pltpu.VMEM((slots, cross), BF),
            pltpu.VMEM((slots, cross), BF),
            pltpu.VMEM((slots, hid), BF),
        ],
        compiler_params=pltpu.CompilerParams(vmem_limit_bytes=54 * 2**20),
        name="score",
    )(
        asked,
        table_slab,
        cross_weight,
        cross_bias,
        hidden_weight,
        hidden_bias.reshape(1, hid),
        out_weight.reshape(1, hid),
    )
    answered = lax.all_to_all(scores, AXES, split_axis=0, concat_axis=0, tiled=True)
    return pl.pallas_call(
        collect_kernel,
        out_shape=jax.ShapeDtypeStruct((groups, width), F32),
        in_specs=[vmem, vmem],
        out_specs=vmem,
        name="collect",
    )(answered, key)


def solution(mesh):
    placed = (
        P("req", "score"),
        P(("req", "score"), None),
        P("req", "score"),
        P(),
        P(),
        P(),
        P(),
        P(),
    )
    return jax.shard_map(
        per_device, mesh=mesh, in_specs=placed, out_specs=P("req", "score"), check_vma=False
    )
```

```python
import jax
import jax.numpy as jnp
from jax import lax
from jax.experimental import pallas as pl
from jax.experimental.pallas import tpu as pltpu
from jax.sharding import PartitionSpec as P

BF = jnp.bfloat16
F32 = jnp.float32
AXES = ("req", "score")
CAP = 8
LANES = 128
WORDS = 4


def iota(shape, axis):
    return lax.broadcasted_iota(jnp.int32, shape, axis)


def in_hbm(array):
    return pltpu.with_memory_space_constraint(array, pltpu.HBM)


def prepare_kernel(
    ids_ref, user_ref, slab_hbm, cross_hbm, msg_ref, key_ref, slab_ref, cross_ref, wide, copied
):
    slab_here = pltpu.make_async_copy(slab_hbm, slab_ref, copied.at[0])
    slab_here.start()
    cross_here = pltpu.make_async_copy(
        cross_hbm.at[0, pl.ds(0, cross_ref.shape[0])], cross_ref, copied.at[1]
    )
    cross_here.start()
    groups, width = ids_ref.shape
    devices = msg_ref.shape[0] // WORDS
    ids = ids_ref[...]
    owner = ids >> 10
    local = ids & 1023
    upto = (iota((width, width), 0) <= iota((width, width), 1)).astype(BF)
    device_row = iota((devices, width), 0)
    base = jnp.zeros((devices, 1), F32)
    high = jnp.zeros((devices, LANES), F32)
    low = jnp.zeros((devices, LANES), F32)
    contract_last = (((1,), (1,)), ((), ()))
    for q in range(groups):
        mine = device_row == owner[q : q + 1, :]
        onehot = mine.astype(BF)
        count = jnp.dot(onehot, upto, preferred_element_type=F32) + base
        rank = jnp.sum(jnp.where(mine, count, 0.0), axis=0, keepdims=True) - 1.0
        rank = rank.astype(jnp.int32)
        base = count[:, width - 1 : width]
        value = local[q : q + 1, :] * groups + (q + 1)
        at_rank = iota((LANES, width), 0) == rank
        value_high = jnp.where(at_rank, value >> 4, 0).astype(F32).astype(BF)
        value_low = jnp.where(at_rank, value & 15, 0).astype(F32).astype(BF)
        high += lax.dot_general(onehot, value_high, contract_last, preferred_element_type=F32)
        low += lax.dot_general(onehot, value_low, contract_last, preferred_element_type=F32)
        key_ref[q : q + 1, :] = owner[q : q + 1, :] * CAP + rank
    user = user_ref[...].astype(F32)
    pairs = [
        jnp.concatenate([user[2 * p : 2 * p + 1, :], user[2 * p + 1 : 2 * p + 2, :]], axis=1)
        for p in range(2)
    ]
    wide[pl.ds(0, devices, stride=WORDS), :] = high
    for p in range(2):
        wide[pl.ds(p + 1, devices, stride=WORDS), :] = jnp.broadcast_to(pairs[p], (devices, LANES))
    wide[pl.ds(3, devices, stride=WORDS), :] = low
    msg_ref[...] = wide[...].astype(BF)
    slab_here.wait()
    cross_here.wait()


def score_kernel(
    msg_ref,
    slab_ref,
    cross_user_ref,
    cross_hbm,
    cross_bias_ref,
    hidden_hbm,
    hidden_bias_ref,
    out_ref,
    score_ref,
    cross_item,
    cross_two,
    hidden_ref,
    copied,
    wide,
    users,
    shift,
    items_hot,
    users_hot,
    first,
    state,
    state_one,
    state_two,
):
    devices = msg_ref.shape[0] // WORDS
    rows = slab_ref.shape[0]
    item_width = slab_ref.shape[1]
    cross = cross_item.shape[1]
    user_width = cross - item_width
    hid = hidden_ref.shape[1]
    slots = CAP * devices
    per_req = devices // 8
    half = slots // 2
    half_ranks = CAP // 2
    tile = 512
    parts = [slice(h, h + half) for h in range(0, slots, half)]

    def tiles(width):
        return [slice(n, n + tile) for n in range(0, width, tile)]

    copies = [
        pltpu.make_async_copy(source, target, copied.at[i])
        for i, (source, target) in enumerate(
            [
                (cross_hbm.at[0, pl.ds(user_width, item_width)], cross_item),
                (cross_hbm.at[1], cross_two),
                (hidden_hbm, hidden_ref),
            ]
        )
    ]
    for copy in copies:
        copy.start()
    cross_item_here, cross_two_here, hidden_here = copies
    wide[...] = msg_ref[...].astype(F32)
    left = iota((8, LANES), 1) < 64
    for t in range(user_width // LANES):
        for p in range(2):
            even = wide[pl.ds(8 * t + 1 + p, 8, stride=WORDS * per_req), :]
            odd = wide[pl.ds(8 * t + 5 + p, 8, stride=WORDS * per_req), :]
            cols = slice(t * LANES, (t + 1) * LANES)
            users[16 * p : 16 * p + 8, cols] = jnp.where(left, even, pltpu.roll(odd, 64, 1))
            users[16 * p + 8 : 16 * p + 16, cols] = jnp.where(left, pltpu.roll(even, 64, 1), odd)
    users_bf = users[...].astype(BF)
    value = wide[pl.ds(0, devices, stride=WORDS), :] * 16.0
    value += wide[pl.ds(3, devices, stride=WORDS), :]
    value = value.astype(jnp.int32) - 1
    row_of = value >> 2
    req_of = (value & 3) * 8 + iota((devices, LANES), 0) // per_req
    row_lane = iota((devices, rows), 1)
    req_lane = iota((devices, LANES), 1)
    for k in range(CAP):
        part = slice(k * devices, (k + 1) * devices)
        items_hot[part, :] = (row_lane == row_of[:, k : k + 1]).astype(BF)
        users_hot[part, :] = ((req_lane & 31) == req_of[:, k : k + 1]).astype(BF)
    for part in parts:
        for cols in tiles(item_width):
            first[part, user_width + cols.start : user_width + cols.stop] = jnp.dot(
                items_hot[part, :], slab_ref[:, cols], preferred_element_type=F32
            ).astype(BF)
    base = jnp.dot(users_bf, cross_user_ref[...], preferred_element_type=F32)
    base = base + (cross_bias_ref[0:1, :] + 1.0)
    base_high = base.astype(BF)
    rest = base - base_high.astype(F32)
    base_mid = rest.astype(BF)
    base_low = (rest - base_mid.astype(F32)).astype(BF)
    shift[0:32, :] = base_high
    shift[32:64, :] = base_mid
    shift[64:96, :] = base_low
    shift[96:128, :] = jnp.zeros_like(base_low)
    for part in parts:
        for cols in tiles(user_width):
            first[part, cols] = jnp.dot(
                users_hot[part, :32], users_bf[:, cols], preferred_element_type=F32
            ).astype(BF)
    cross_item_here.wait()
    for part in parts:
        for cols in tiles(cross):
            factor = jnp.dot(
                first[part, user_width:],
                cross_item[:, cols],
                preferred_element_type=F32,
            )
            factor += jnp.dot(users_hot[part, :], shift[:, cols], preferred_element_type=F32)
            new = first[part, cols].astype(F32) * factor
            state[part, cols] = new
            state_one[part, cols] = new.astype(BF)
    cross_two_here.wait()
    for part in parts:
        for cols in tiles(cross):
            mixed = jnp.dot(
                state_one[part, :], cross_two[:, cols], preferred_element_type=F32
            )
            mixed += cross_bias_ref[1:2, cols]
            new = first[part, cols].astype(F32) * mixed + state[part, cols]
            state_two[part, cols] = new.astype(BF)
    hidden_here.wait()
    lane = iota((devices, LANES), 1)
    total = jnp.zeros((devices, LANES), F32)
    for part in range(2):
        gathered = jnp.zeros((half, LANES), F32)
        for start in range(0, hid, tile):
            cols = slice(start, start + tile)
            hidden = jnp.dot(
                state_two[part * half : (part + 1) * half, :],
                hidden_ref[:, cols],
                preferred_element_type=F32,
            )
            for j in range(tile // LANES):
                at = start // LANES + j
                unit = hidden[:, j * LANES : (j + 1) * LANES] + hidden_bias_ref[at : at + 1, :]
                unit = jnp.maximum(unit, 0.0).astype(BF).astype(F32)
                gathered += unit * out_ref[at : at + 1, :].astype(F32)
        logit = jnp.sum(gathered, axis=1, keepdims=True)
        for k in range(half_ranks):
            here = lane == part * half_ranks + k
            total = jnp.where(here, logit[k * devices : (k + 1) * devices, :], total)
    score_ref[...] = jax.nn.sigmoid(total)


def collect_kernel(scores_ref, key_ref, out_ref):
    groups, width = key_ref.shape
    devices = scores_ref.shape[0]
    scores = scores_ref[...]
    for q in range(groups):
        key = key_ref[q : q + 1, :]
        total = jnp.zeros((devices, width), F32)
        for k in range(CAP):
            here = iota((devices, width), 0) * CAP + k == key
            total += jnp.where(here, scores[:, k : k + 1], 0.0)
        out_ref[q : q + 1, :] = jnp.sum(total, axis=0, keepdims=True)


def per_device(
    cand_ids,
    table_slab,
    user_rows,
    cross_weight,
    cross_bias,
    hidden_weight,
    hidden_bias,
    out_weight,
):
    devices = lax.axis_size("req") * lax.axis_size("score")
    groups, width = cand_ids.shape
    slots = devices * CAP
    cross = cross_weight.shape[1]
    hid = hidden_weight.shape[1]
    vmem = pl.BlockSpec(memory_space=pltpu.VMEM)
    hbm = pl.BlockSpec(memory_space=pl.ANY)
    item_width = table_slab.shape[1]
    user_width = cross - item_width
    in_vmem = pltpu.with_memory_space_constraint
    msg, key, slab, cross_user = pl.pallas_call(
        prepare_kernel,
        out_shape=(
            jax.ShapeDtypeStruct((devices * WORDS, LANES), BF),
            jax.ShapeDtypeStruct((groups, width), jnp.int32),
            pltpu.VMEM(table_slab.shape, BF),
            pltpu.VMEM((user_width, cross), BF),
        ),
        in_specs=[vmem, vmem, hbm, hbm],
        out_specs=(vmem, vmem, vmem, vmem),
        scratch_shapes=[
            pltpu.VMEM((devices * WORDS, LANES), F32),
            pltpu.SemaphoreType.DMA((2,)),
        ],
        compiler_params=pltpu.CompilerParams(vmem_limit_bytes=16 * 2**20),
        name="prepare",
    )(in_hbm(cand_ids), in_hbm(user_rows), in_hbm(table_slab), in_hbm(cross_weight))
    asked = lax.all_to_all(msg, AXES, split_axis=0, concat_axis=0, tiled=True)
    scores = pl.pallas_call(
        score_kernel,
        out_shape=pltpu.VMEM((devices, LANES), F32),
        in_specs=[vmem, vmem, vmem, hbm, vmem, hbm, vmem, vmem],
        out_specs=vmem,
        scratch_shapes=[
            pltpu.VMEM((item_width, cross), BF),
            pltpu.VMEM((cross, cross), BF),
            pltpu.VMEM((cross, hid), BF),
            pltpu.SemaphoreType.DMA((3,)),
            pltpu.VMEM((devices * WORDS, LANES), F32),
            pltpu.VMEM((32, user_width), F32),
            pltpu.VMEM((LANES, cross), BF),
            pltpu.VMEM((slots, table_slab.shape[0]), BF),
            pltpu.VMEM((slots, LANES), BF),
            pltpu.VMEM((slots, cross), BF),
            pltpu.VMEM((slots, cross), F32),
            pltpu.VMEM((slots, cross), BF),
            pltpu.VMEM((slots, cross), BF),
        ],
        compiler_params=pltpu.CompilerParams(vmem_limit_bytes=50 * 2**20),
        name="score",
    )(
        asked,
        in_vmem(slab, pltpu.VMEM),
        in_vmem(cross_user, pltpu.VMEM),
        in_hbm(cross_weight),
        cross_bias,
        in_hbm(hidden_weight),
        hidden_bias.reshape(hid // LANES, LANES),
        out_weight.reshape(hid // LANES, LANES),
    )
    answered = lax.all_to_all(scores, AXES, split_axis=0, concat_axis=0, tiled=True)
    return pl.pallas_call(
        collect_kernel,
        out_shape=jax.ShapeDtypeStruct((groups, width), F32),
        in_specs=[vmem, vmem],
        out_specs=vmem,
        name="collect",
    )(answered, key)


def solution(mesh):
    placed = (
        P("req", "score"),
        P(("req", "score"), None),
        P("req", "score"),
        P(),
        P(),
        P(),
        P(),
        P(),
    )
    return jax.shard_map(
        per_device, mesh=mesh, in_specs=placed, out_specs=P("req", "score"), check_vma=False
    )
```

```python
import jax
import jax.numpy as jnp
from jax import lax
from jax.experimental import pallas as pl
from jax.experimental.pallas import tpu as pltpu
from jax.sharding import PartitionSpec as P

BF = jnp.bfloat16
F32 = jnp.float32
AXES = ("req", "score")
CAP = 8
LANES = 128
WORDS = 4


def iota(shape, axis):
    return lax.broadcasted_iota(jnp.int32, shape, axis)


def in_hbm(array):
    return pltpu.with_memory_space_constraint(array, pltpu.HBM)


def prepare_kernel(
    ids_ref, user_ref, slab_hbm, msg_ref, key_ref, slab_ref, wide, copied
):
    slab_here = pltpu.make_async_copy(
        slab_hbm.at[:, pl.ds(0, slab_ref.shape[1])], slab_ref, copied
    )
    slab_here.start()
    groups, width = ids_ref.shape
    devices = msg_ref.shape[0] // WORDS
    ids = ids_ref[...]
    owner = ids >> 10
    local = ids & 1023
    upto = (iota((width, width), 0) <= iota((width, width), 1)).astype(BF)
    device_row = iota((devices, width), 0)
    base = jnp.zeros((devices, 1), F32)
    high = jnp.zeros((devices, LANES), F32)
    low = jnp.zeros((devices, LANES), F32)
    contract_last = (((1,), (1,)), ((), ()))
    for q in range(groups):
        mine = device_row == owner[q : q + 1, :]
        onehot = mine.astype(BF)
        count = jnp.dot(onehot, upto, preferred_element_type=F32) + base
        rank = jnp.sum(jnp.where(mine, count, 0.0), axis=0, keepdims=True) - 1.0
        rank = rank.astype(jnp.int32)
        base = count[:, width - 1 : width]
        value = local[q : q + 1, :] * groups + (q + 1)
        at_rank = iota((LANES, width), 0) == rank
        value_high = jnp.where(at_rank, value >> 4, 0).astype(F32).astype(BF)
        value_low = jnp.where(at_rank, value & 15, 0).astype(F32).astype(BF)
        high += lax.dot_general(onehot, value_high, contract_last, preferred_element_type=F32)
        low += lax.dot_general(onehot, value_low, contract_last, preferred_element_type=F32)
        key_ref[q : q + 1, :] = owner[q : q + 1, :] * CAP + rank
    user = user_ref[...].astype(F32)
    pairs = [
        jnp.concatenate([user[2 * p : 2 * p + 1, :], user[2 * p + 1 : 2 * p + 2, :]], axis=1)
        for p in range(2)
    ]
    wide[pl.ds(0, devices, stride=WORDS), :] = high
    for p in range(2):
        wide[pl.ds(p + 1, devices, stride=WORDS), :] = jnp.broadcast_to(pairs[p], (devices, LANES))
    wide[pl.ds(3, devices, stride=WORDS), :] = low
    msg_ref[...] = wide[...].astype(BF)
    slab_here.wait()


def score_kernel(
    msg_ref,
    slab_ref,
    slab_hbm,
    cross_hbm,
    cross_bias_ref,
    hidden_hbm,
    hidden_bias_ref,
    out_ref,
    score_ref,
    slab_rest,
    cross_user,
    cross_item,
    cross_two,
    hidden_ref,
    copied,
    wide,
    users,
    shift,
    items_hot,
    users_hot,
    first,
    state,
    state_one,
    state_two,
):
    devices = msg_ref.shape[0] // WORDS
    rows = slab_ref.shape[0]
    staged = slab_ref.shape[1]
    item_width = staged + slab_rest.shape[1]
    cross = cross_item.shape[1]
    user_width = cross - item_width
    hid = hidden_ref.shape[1]
    slots = CAP * devices
    per_req = devices // 8
    half = slots // 2
    half_ranks = CAP // 2
    tile = 512
    parts = [slice(h, h + half) for h in range(0, slots, half)]

    def tiles(width):
        return [slice(n, n + tile) for n in range(0, width, tile)]

    copies = [
        pltpu.make_async_copy(source, target, copied.at[i])
        for i, (source, target) in enumerate(
            [
                (slab_hbm.at[:, pl.ds(staged, item_width - staged)], slab_rest),
                (cross_hbm.at[0, pl.ds(0, user_width)], cross_user),
                (cross_hbm.at[0, pl.ds(user_width, item_width)], cross_item),
                (cross_hbm.at[1], cross_two),
                (hidden_hbm, hidden_ref),
            ]
        )
    ]
    for copy in copies:
        copy.start()
    slab_here, cross_user_here, cross_item_here, cross_two_here, hidden_here = copies
    wide[...] = msg_ref[...].astype(F32)
    left = iota((8, LANES), 1) < 64
    for t in range(user_width // LANES):
        for p in range(2):
            even = wide[pl.ds(8 * t + 1 + p, 8, stride=WORDS * per_req), :]
            odd = wide[pl.ds(8 * t + 5 + p, 8, stride=WORDS * per_req), :]
            cols = slice(t * LANES, (t + 1) * LANES)
            users[16 * p : 16 * p + 8, cols] = jnp.where(left, even, pltpu.roll(odd, 64, 1))
            users[16 * p + 8 : 16 * p + 16, cols] = jnp.where(left, pltpu.roll(even, 64, 1), odd)
    users_bf = users[...].astype(BF)
    value = wide[pl.ds(0, devices, stride=WORDS), :] * 16.0
    value += wide[pl.ds(3, devices, stride=WORDS), :]
    value = value.astype(jnp.int32) - 1
    row_of = value >> 2
    req_of = (value & 3) * 8 + iota((devices, LANES), 0) // per_req
    row_lane = iota((devices, rows), 1)
    req_lane = iota((devices, LANES), 1)
    for k in range(CAP):
        part = slice(k * devices, (k + 1) * devices)
        items_hot[part, :] = (row_lane == row_of[:, k : k + 1]).astype(BF)
        users_hot[part, :] = ((req_lane & 31) == req_of[:, k : k + 1]).astype(BF)
    for table, at in ((slab_ref, user_width), (slab_rest, user_width + staged)):
        if table is slab_rest:
            slab_here.wait()
        for part in parts:
            for cols in tiles(table.shape[1]):
                first[part, at + cols.start : at + cols.stop] = jnp.dot(
                    items_hot[part, :], table[:, cols], preferred_element_type=F32
                ).astype(BF)
    cross_user_here.wait()
    base = jnp.dot(users_bf, cross_user[...], preferred_element_type=F32)
    base = base + (cross_bias_ref[0:1, :] + 1.0)
    base_high = base.astype(BF)
    rest = base - base_high.astype(F32)
    base_mid = rest.astype(BF)
    base_low = (rest - base_mid.astype(F32)).astype(BF)
    shift[0:32, :] = base_high
    shift[32:64, :] = base_mid
    shift[64:96, :] = base_low
    shift[96:128, :] = jnp.zeros_like(base_low)
    for part in parts:
        for cols in tiles(user_width):
            first[part, cols] = jnp.dot(
                users_hot[part, :32], users_bf[:, cols], preferred_element_type=F32
            ).astype(BF)
    cross_item_here.wait()
    for part in parts:
        for cols in tiles(cross):
            factor = jnp.dot(
                first[part, user_width:],
                cross_item[:, cols],
                preferred_element_type=F32,
            )
            factor += jnp.dot(users_hot[part, :], shift[:, cols], preferred_element_type=F32)
            new = first[part, cols].astype(F32) * factor
            state[part, cols] = new
            state_one[part, cols] = new.astype(BF)
    cross_two_here.wait()
    for part in parts:
        for cols in tiles(cross):
            mixed = jnp.dot(
                state_one[part, :], cross_two[:, cols], preferred_element_type=F32
            )
            mixed += cross_bias_ref[1:2, cols]
            new = first[part, cols].astype(F32) * mixed + state[part, cols]
            state_two[part, cols] = new.astype(BF)
    hidden_here.wait()
    lane = iota((devices, LANES), 1)
    total = jnp.zeros((devices, LANES), F32)
    for part in range(2):
        gathered = jnp.zeros((half, LANES), F32)
        for start in range(0, hid, tile):
            cols = slice(start, start + tile)
            hidden = jnp.dot(
                state_two[part * half : (part + 1) * half, :],
                hidden_ref[:, cols],
                preferred_element_type=F32,
            )
            for j in range(tile // LANES):
                at = start // LANES + j
                unit = hidden[:, j * LANES : (j + 1) * LANES] + hidden_bias_ref[at : at + 1, :]
                unit = jnp.maximum(unit, 0.0).astype(BF).astype(F32)
                gathered += unit * out_ref[at : at + 1, :].astype(F32)
        logit = jnp.sum(gathered, axis=1, keepdims=True)
        for k in range(half_ranks):
            here = lane == part * half_ranks + k
            total = jnp.where(here, logit[k * devices : (k + 1) * devices, :], total)
    score_ref[...] = jax.nn.sigmoid(total)


def collect_kernel(scores_ref, key_ref, out_ref):
    groups, width = key_ref.shape
    devices = scores_ref.shape[0]
    scores = scores_ref[...]
    for q in range(groups):
        key = key_ref[q : q + 1, :]
        total = jnp.zeros((devices, width), F32)
        for k in range(CAP):
            here = iota((devices, width), 0) * CAP + k == key
            total += jnp.where(here, scores[:, k : k + 1], 0.0)
        out_ref[q : q + 1, :] = jnp.sum(total, axis=0, keepdims=True)


def per_device(
    cand_ids,
    table_slab,
    user_rows,
    cross_weight,
    cross_bias,
    hidden_weight,
    hidden_bias,
    out_weight,
):
    devices = lax.axis_size("req") * lax.axis_size("score")
    groups, width = cand_ids.shape
    slots = devices * CAP
    cross = cross_weight.shape[1]
    hid = hidden_weight.shape[1]
    vmem = pl.BlockSpec(memory_space=pltpu.VMEM)
    hbm = pl.BlockSpec(memory_space=pl.ANY)
    item_width = table_slab.shape[1]
    user_width = cross - item_width
    in_vmem = pltpu.with_memory_space_constraint
    staged = item_width // 2
    msg, key, slab = pl.pallas_call(
        prepare_kernel,
        out_shape=(
            jax.ShapeDtypeStruct((devices * WORDS, LANES), BF),
            jax.ShapeDtypeStruct((groups, width), jnp.int32),
            pltpu.VMEM((table_slab.shape[0], staged), BF),
        ),
        in_specs=[vmem, vmem, hbm],
        out_specs=(vmem, vmem, vmem),
        scratch_shapes=[
            pltpu.VMEM((devices * WORDS, LANES), F32),
            pltpu.SemaphoreType.DMA,
        ],
        compiler_params=pltpu.CompilerParams(vmem_limit_bytes=16 * 2**20),
        name="prepare",
    )(in_hbm(cand_ids), in_hbm(user_rows), in_hbm(table_slab))
    asked = lax.all_to_all(msg, AXES, split_axis=0, concat_axis=0, tiled=True)
    scores = pl.pallas_call(
        score_kernel,
        out_shape=pltpu.VMEM((devices, LANES), F32),
        in_specs=[vmem, vmem, hbm, hbm, vmem, hbm, vmem, vmem],
        out_specs=vmem,
        scratch_shapes=[
            pltpu.VMEM((table_slab.shape[0], item_width - staged), BF),
            pltpu.VMEM((user_width, cross), BF),
            pltpu.VMEM((item_width, cross), BF),
            pltpu.VMEM((cross, cross), BF),
            pltpu.VMEM((cross, hid), BF),
            pltpu.SemaphoreType.DMA((5,)),
            pltpu.VMEM((devices * WORDS, LANES), F32),
            pltpu.VMEM((32, user_width), F32),
            pltpu.VMEM((LANES, cross), BF),
            pltpu.VMEM((slots, table_slab.shape[0]), BF),
            pltpu.VMEM((slots, LANES), BF),
            pltpu.VMEM((slots, cross), BF),
            pltpu.VMEM((slots, cross), F32),
            pltpu.VMEM((slots, cross), BF),
            pltpu.VMEM((slots, cross), BF),
        ],
        compiler_params=pltpu.CompilerParams(vmem_limit_bytes=50 * 2**20),
        name="score",
    )(
        asked,
        in_vmem(slab, pltpu.VMEM),
        in_hbm(table_slab),
        in_hbm(cross_weight),
        in_hbm(cross_bias),
        in_hbm(hidden_weight),
        in_hbm(hidden_bias.reshape(hid // LANES, LANES)),
        in_hbm(out_weight.reshape(hid // LANES, LANES)),
    )
    answered = lax.all_to_all(scores, AXES, split_axis=0, concat_axis=0, tiled=True)
    return pl.pallas_call(
        collect_kernel,
        out_shape=jax.ShapeDtypeStruct((groups, width), F32),
        in_specs=[vmem, vmem],
        out_specs=vmem,
        compiler_params=pltpu.CompilerParams(vmem_limit_bytes=2 * 2**20),
        name="collect",
    )(answered, key)


def solution(mesh):
    placed = (
        P("req", "score"),
        P(("req", "score"), None),
        P("req", "score"),
        P(),
        P(),
        P(),
        P(),
        P(),
    )
    return jax.shard_map(
        per_device, mesh=mesh, in_specs=placed, out_specs=P("req", "score"), check_vma=False
    )
```

```python
import jax
import jax.numpy as jnp
from jax import lax
from jax.experimental import pallas as pl
from jax.experimental.pallas import tpu as pltpu
from jax.sharding import PartitionSpec as P

BF = jnp.bfloat16
F32 = jnp.float32
AXES = ("req", "score")
CAP = 8
LANES = 128
WORDS = 4


def iota(shape, axis):
    return lax.broadcasted_iota(jnp.int32, shape, axis)


def in_hbm(array):
    return pltpu.with_memory_space_constraint(array, pltpu.HBM)


def prepare_kernel(
    ids_ref, user_ref, slab_hbm, msg_ref, key_ref, slab_ref, wide, copied
):
    slab_here = pltpu.make_async_copy(
        slab_hbm.at[:, pl.ds(0, slab_ref.shape[1])], slab_ref, copied
    )
    slab_here.start()
    groups, width = ids_ref.shape
    devices = msg_ref.shape[0] // WORDS
    ids = ids_ref[...]
    owner = ids >> 10
    local = ids & 1023
    upto = (iota((width, width), 0) <= iota((width, width), 1)).astype(BF)
    device_row = iota((devices, width), 0)
    base = jnp.zeros((devices, 1), F32)
    high = jnp.zeros((devices, LANES), F32)
    low = jnp.zeros((devices, LANES), F32)
    contract_last = (((1,), (1,)), ((), ()))
    for q in range(groups):
        mine = device_row == owner[q : q + 1, :]
        onehot = mine.astype(BF)
        count = jnp.dot(onehot, upto, preferred_element_type=F32) + base
        rank = jnp.sum(jnp.where(mine, count, 0.0), axis=0, keepdims=True) - 1.0
        rank = rank.astype(jnp.int32)
        base = count[:, width - 1 : width]
        value = local[q : q + 1, :] * groups + (q + 1)
        at_rank = iota((LANES, width), 0) == rank
        value_high = jnp.where(at_rank, value >> 4, 0).astype(F32).astype(BF)
        value_low = jnp.where(at_rank, value & 15, 0).astype(F32).astype(BF)
        high += lax.dot_general(onehot, value_high, contract_last, preferred_element_type=F32)
        low += lax.dot_general(onehot, value_low, contract_last, preferred_element_type=F32)
        key_ref[q : q + 1, :] = owner[q : q + 1, :] * CAP + rank
    user = user_ref[...].astype(F32)
    pairs = [
        jnp.concatenate([user[2 * p : 2 * p + 1, :], user[2 * p + 1 : 2 * p + 2, :]], axis=1)
        for p in range(2)
    ]
    wide[pl.ds(0, devices, stride=WORDS), :] = high
    for p in range(2):
        wide[pl.ds(p + 1, devices, stride=WORDS), :] = jnp.broadcast_to(pairs[p], (devices, LANES))
    wide[pl.ds(3, devices, stride=WORDS), :] = low
    msg_ref[...] = wide[...].astype(BF)
    slab_here.wait()


def score_kernel(
    msg_ref,
    slab_ref,
    slab_hbm,
    cross_hbm,
    cross_bias_ref,
    hidden_hbm,
    hidden_bias_ref,
    out_ref,
    score_ref,
    slab_rest,
    cross_user,
    cross_item,
    cross_two,
    hidden_ref,
    copied,
    wide,
    users,
    shift,
    request,
    items_hot,
    first,
    state,
    state_one,
    state_two,
):
    devices = msg_ref.shape[0] // WORDS
    rows = slab_ref.shape[0]
    staged = slab_ref.shape[1]
    item_width = staged + slab_rest.shape[1]
    cross = cross_item.shape[1]
    user_width = cross - item_width
    hid = hidden_ref.shape[1]
    slots = CAP * devices
    per_req = devices // 8
    half = slots // 2
    half_ranks = CAP // 2
    tile = 512
    parts = [slice(h, h + half) for h in range(0, slots, half)]

    def tiles(width):
        return [slice(n, n + tile) for n in range(0, width, tile)]

    def copy(i, source, target):
        return pltpu.make_async_copy(source, target, copied.at[i])

    columns = tiles(cross)
    count = len(columns)
    slab_here = copy(0, slab_hbm.at[:, pl.ds(staged, item_width - staged)], slab_rest)
    cross_two_here = copy(1, cross_hbm.at[1], cross_two)
    hidden_here = copy(2, hidden_hbm, hidden_ref)
    user_here, item_here = [], []
    for n, cols in enumerate(columns):
        cols = pl.ds(cols.start, tile)
        user_here.append(
            copy(3 + n, cross_hbm.at[0, pl.ds(0, user_width), cols], cross_user.at[:, cols])
        )
        item_here.append(
            copy(
                3 + count + n,
                cross_hbm.at[0, pl.ds(user_width, item_width), cols],
                cross_item.at[:, cols],
            )
        )
    slab_here.start()
    for n in range(count):
        user_here[n].start()
        item_here[n].start()
    wide[...] = msg_ref[...].astype(F32)

    def fetch(part, table, at):
        for cols in tiles(table.shape[1]):
            first[part, at + cols.start : at + cols.stop] = jnp.dot(
                items_hot[part, :], table[:, cols], preferred_element_type=F32
            ).astype(BF)

    value = wide[pl.ds(0, devices, stride=WORDS), :] * 16.0
    value += wide[pl.ds(3, devices, stride=WORDS), :]
    value = value.astype(jnp.int32) - 1
    row_of = value >> 2
    req_of = (value & 3) + (iota((devices, LANES), 0) // per_req & 1) * 4
    row_lane = iota((devices, rows), 1)
    for part in parts:
        for k in range(part.start // devices, part.stop // devices):
            here = slice(k * devices, (k + 1) * devices)
            items_hot[here, :] = (row_lane == row_of[:, k : k + 1]).astype(BF)
            request[here, :] = jnp.broadcast_to(req_of[:, k : k + 1], (devices, LANES))
        fetch(part, slab_ref, user_width)
    left = iota((8, LANES), 1) < 64
    for t in range(user_width // LANES):
        for p in range(2):
            even = wide[pl.ds(8 * t + 1 + p, 8, stride=WORDS * per_req), :]
            odd = wide[pl.ds(8 * t + 5 + p, 8, stride=WORDS * per_req), :]
            users[t, pl.ds(2 * p, 8, stride=4), :] = jnp.where(left, even, pltpu.roll(odd, 64, 1))
            users[t, pl.ds(2 * p + 1, 8, stride=4), :] = jnp.where(
                left, pltpu.roll(even, 64, 1), odd
            )
    slab_here.wait()
    for part in parts:
        fetch(part, slab_rest, user_width + staged)
    users_bf = jnp.concatenate(
        [users[t].astype(BF) for t in range(user_width // LANES)], axis=1
    )
    along_rows = lax.GatherDimensionNumbers(
        offset_dims=(),
        collapsed_slice_dims=(0,),
        start_index_map=(0,),
        operand_batching_dims=(1,),
        start_indices_batching_dims=(1,),
    )

    def of_request(rows, places):
        got = [
            lax.gather(
                rows,
                place,
                along_rows,
                slice_sizes=(1, 1),
                mode=lax.GatherScatterMode.PROMISE_IN_BOUNDS,
            )
            for place in places
        ]
        return jnp.concatenate(got, axis=0)

    def request_term(n):
        user_here[n].wait()
        item_here[n].wait()
        cols = columns[n]
        base = jnp.dot(users_bf, cross_user[:, cols], preferred_element_type=F32)
        shift[:, cols] = base + (cross_bias_ref[0:1, cols] + 1.0)

    def layer_one(part, cols):
        mixed = jnp.dot(first[part, user_width:], cross_item[:, cols], preferred_element_type=F32)
        for start in range(cols.start, cols.stop, LANES):
            lanes = slice(start, start + LANES)
            for at in range(part.start, part.stop, per_req):
                here = slice(at, at + per_req)
                pair = at % devices // per_req // 2 * 8
                places = [request[n : n + 8, :][:, :, None] for n in (at, at + 8)]
                factor = mixed[
                    at - part.start : at - part.start + per_req,
                    start - cols.start : start - cols.start + LANES,
                ]
                factor = factor + of_request(shift[pair : pair + 8, lanes], places)
                if start < user_width:
                    own = of_request(users[start // LANES, pair : pair + 8, :], places)
                    first[here, lanes] = own.astype(BF)
                else:
                    own = first[here, lanes].astype(F32)
                new = own * factor
                state[here, lanes] = new
                state_one[here, lanes] = new.astype(BF)

    request_term(0)
    for n, cols in enumerate(columns):
        layer_one(parts[0], cols)
        if n + 1 < count:
            request_term(n + 1)
        else:
            cross_two_here.wait()
            hidden_here.start()
        if n == 0:
            cross_two_here.start()
        layer_one(parts[1], cols)
    for part in parts:
        if part.start > 0:
            hidden_here.wait()
        for cols in tiles(cross):
            mixed = jnp.dot(state_one[part, :], cross_two[:, cols], preferred_element_type=F32)
            mixed += cross_bias_ref[1:2, cols]
            new = first[part, cols].astype(F32) * mixed + state[part, cols]
            state_two[part, cols] = new.astype(BF)
    lane = iota((devices, LANES), 1)
    total = jnp.zeros((devices, LANES), F32)
    for part in range(2):
        gathered = jnp.zeros((half, LANES), F32)
        for start in range(0, hid, tile):
            cols = slice(start, start + tile)
            hidden = jnp.dot(
                state_two[part * half : (part + 1) * half, :],
                hidden_ref[:, cols],
                preferred_element_type=F32,
            )
            for j in range(tile // LANES):
                at = start // LANES + j
                unit = hidden[:, j * LANES : (j + 1) * LANES] + hidden_bias_ref[at : at + 1, :]
                unit = jnp.maximum(unit, 0.0).astype(BF).astype(F32)
                gathered += unit * out_ref[at : at + 1, :].astype(F32)
        logit = jnp.sum(gathered, axis=1, keepdims=True)
        for k in range(half_ranks):
            here = lane == part * half_ranks + k
            total = jnp.where(here, logit[k * devices : (k + 1) * devices, :], total)
    score_ref[...] = jax.nn.sigmoid(total)


def collect_kernel(scores_ref, key_ref, out_ref):
    groups, width = key_ref.shape
    devices = scores_ref.shape[0]
    scores = scores_ref[...]
    for q in range(groups):
        key = key_ref[q : q + 1, :]
        total = jnp.zeros((devices, width), F32)
        for k in range(CAP):
            here = iota((devices, width), 0) * CAP + k == key
            total += jnp.where(here, scores[:, k : k + 1], 0.0)
        out_ref[q : q + 1, :] = jnp.sum(total, axis=0, keepdims=True)


def per_device(
    cand_ids,
    table_slab,
    user_rows,
    cross_weight,
    cross_bias,
    hidden_weight,
    hidden_bias,
    out_weight,
):
    devices = lax.axis_size("req") * lax.axis_size("score")
    groups, width = cand_ids.shape
    slots = devices * CAP
    cross = cross_weight.shape[1]
    hid = hidden_weight.shape[1]
    vmem = pl.BlockSpec(memory_space=pltpu.VMEM)
    hbm = pl.BlockSpec(memory_space=pl.ANY)
    item_width = table_slab.shape[1]
    user_width = cross - item_width
    in_vmem = pltpu.with_memory_space_constraint
    staged = item_width // 2
    msg, key, slab = pl.pallas_call(
        prepare_kernel,
        out_shape=(
            jax.ShapeDtypeStruct((devices * WORDS, LANES), BF),
            jax.ShapeDtypeStruct((groups, width), jnp.int32),
            pltpu.VMEM((table_slab.shape[0], staged), BF),
        ),
        in_specs=[vmem, vmem, hbm],
        out_specs=(vmem, vmem, vmem),
        scratch_shapes=[
            pltpu.VMEM((devices * WORDS, LANES), F32),
            pltpu.SemaphoreType.DMA,
        ],
        compiler_params=pltpu.CompilerParams(vmem_limit_bytes=16 * 2**20),
        name="prepare",
    )(in_hbm(cand_ids), in_hbm(user_rows), in_hbm(table_slab))
    asked = lax.all_to_all(msg, AXES, split_axis=0, concat_axis=0, tiled=True)
    scores = pl.pallas_call(
        score_kernel,
        out_shape=pltpu.VMEM((devices, LANES), F32),
        in_specs=[vmem, vmem, hbm, hbm, vmem, hbm, vmem, vmem],
        out_specs=vmem,
        scratch_shapes=[
            pltpu.VMEM((table_slab.shape[0], item_width - staged), BF),
            pltpu.VMEM((user_width, cross), BF),
            pltpu.VMEM((item_width, cross), BF),
            pltpu.VMEM((cross, cross), BF),
            pltpu.VMEM((cross, hid), BF),
            pltpu.SemaphoreType.DMA((11,)),
            pltpu.VMEM((devices * WORDS, LANES), F32),
            pltpu.VMEM((user_width // LANES, 32, LANES), F32),
            pltpu.VMEM((32, cross), F32),
            pltpu.VMEM((slots, LANES), jnp.int32),
            pltpu.VMEM((slots, table_slab.shape[0]), BF),
            pltpu.VMEM((slots, cross), BF),
            pltpu.VMEM((slots, cross), F32),
            pltpu.VMEM((slots, cross), BF),
            pltpu.VMEM((slots, cross), BF),
        ],
        compiler_params=pltpu.CompilerParams(vmem_limit_bytes=50 * 2**20),
        name="score",
    )(
        asked,
        in_vmem(slab, pltpu.VMEM),
        in_hbm(table_slab),
        in_hbm(cross_weight),
        in_hbm(cross_bias),
        in_hbm(hidden_weight),
        in_hbm(hidden_bias.reshape(hid // LANES, LANES)),
        in_hbm(out_weight.reshape(hid // LANES, LANES)),
    )
    answered = lax.all_to_all(scores, AXES, split_axis=0, concat_axis=0, tiled=True)
    return pl.pallas_call(
        collect_kernel,
        out_shape=jax.ShapeDtypeStruct((groups, width), F32),
        in_specs=[vmem, vmem],
        out_specs=vmem,
        compiler_params=pltpu.CompilerParams(vmem_limit_bytes=2 * 2**20),
        name="collect",
    )(answered, key)


def solution(mesh):
    placed = (
        P("req", "score"),
        P(("req", "score"), None),
        P("req", "score"),
        P(),
        P(),
        P(),
        P(),
        P(),
    )
    return jax.shard_map(
        per_device, mesh=mesh, in_specs=placed, out_specs=P("req", "score"), check_vma=False
    )
```

```python
import jax
import jax.numpy as jnp
from jax import lax
from jax.experimental import pallas as pl
from jax.experimental.pallas import tpu as pltpu
from jax.sharding import PartitionSpec as P

BF = jnp.bfloat16
F32 = jnp.float32
AXES = ("req", "score")
CAP = 8
LANES = 128
WORDS = 4


def iota(shape, axis):
    return lax.broadcasted_iota(jnp.int32, shape, axis)


def in_hbm(array):
    return pltpu.with_memory_space_constraint(array, pltpu.HBM)


def prepare_kernel(
    ids_hbm,
    user_hbm,
    slab_hbm,
    msg_ref,
    key_ref,
    slab_ref,
    ids_ref,
    user_ref,
    wide,
    copied,
):
    ids_here = pltpu.make_async_copy(ids_hbm, ids_ref, copied.at[0])
    user_here = pltpu.make_async_copy(user_hbm, user_ref, copied.at[1])
    slab_here = pltpu.make_async_copy(
        slab_hbm.at[:, pl.ds(0, slab_ref.shape[1])], slab_ref, copied.at[2]
    )
    ids_here.start()
    user_here.start()
    slab_here.start()
    ids_here.wait()
    groups, width = ids_ref.shape
    devices = msg_ref.shape[0] // WORDS
    ids = ids_ref[...]
    owner = ids >> 10
    local = ids & 1023
    upto = (iota((width, width), 0) <= iota((width, width), 1)).astype(BF)
    device_row = iota((devices, width), 0)
    base = jnp.zeros((devices, 1), F32)
    slot_values = jnp.zeros((devices, LANES), F32)
    contract_last = (((1,), (1,)), ((), ()))
    for q in range(groups):
        mine = device_row == owner[q : q + 1, :]
        onehot = mine.astype(BF)
        count = jnp.dot(onehot, upto, preferred_element_type=F32) + base
        rank = jnp.sum(jnp.where(mine, count, 0.0), axis=0, keepdims=True) - 1.0
        rank = rank.astype(jnp.int32)
        base = count[:, width - 1 : width]
        value = local[q : q + 1, :] * groups + (q + 1)
        place = iota((LANES, width), 0)
        digit = jnp.where(place == rank, value >> 4, 0)
        digit = jnp.where(place == rank + CAP, value & 15, digit)
        slot_values += lax.dot_general(
            onehot, digit.astype(F32).astype(BF), contract_last, preferred_element_type=F32
        )
        key_ref[q : q + 1, :] = owner[q : q + 1, :] * CAP + rank
    user_here.wait()
    user = user_ref[...].astype(F32)
    pairs = [
        jnp.concatenate([user[2 * p : 2 * p + 1, :], user[2 * p + 1 : 2 * p + 2, :]], axis=1)
        for p in range(2)
    ]
    wide[pl.ds(0, devices, stride=WORDS), :] = slot_values
    for p in range(2):
        wide[pl.ds(p + 1, devices, stride=WORDS), :] = jnp.broadcast_to(pairs[p], (devices, LANES))
    wide[pl.ds(3, devices, stride=WORDS), :] = jnp.zeros((devices, LANES), F32)
    msg_ref[...] = wide[...].astype(BF)
    slab_here.wait()


def score_kernel(
    msg_ref,
    slab_ref,
    slab_hbm,
    cross_hbm,
    cross_bias_ref,
    hidden_hbm,
    hidden_bias_ref,
    out_ref,
    score_ref,
    slab_rest,
    cross_user,
    cross_item,
    cross_two,
    hidden_ref,
    copied,
    wide,
    users,
    shift,
    request,
    items_hot,
    first,
    state,
    state_one,
    state_two,
):
    devices = msg_ref.shape[0] // WORDS
    rows = slab_ref.shape[0]
    staged = slab_ref.shape[1]
    item_width = staged + slab_rest.shape[1]
    cross = cross_item.shape[1]
    user_width = cross - item_width
    hid = hidden_ref.shape[1]
    slots = CAP * devices
    per_req = devices // 8
    half = slots // 2
    half_ranks = CAP // 2
    tile = 512
    parts = [slice(h, h + half) for h in range(0, slots, half)]

    def tiles(width, size=tile):
        return [slice(n, n + size) for n in range(0, width, size)]

    def copy(i, source, target):
        return pltpu.make_async_copy(source, target, copied.at[i])

    columns = tiles(cross)
    count = len(columns)
    slab_here = copy(0, slab_hbm.at[:, pl.ds(staged, item_width - staged)], slab_rest)
    cross_two_here = copy(1, cross_hbm.at[1], cross_two)
    hidden_here = copy(2, hidden_hbm, hidden_ref)
    user_here, item_here = [], []
    for n, cols in enumerate(columns):
        cols = pl.ds(cols.start, tile)
        user_here.append(
            copy(3 + n, cross_hbm.at[0, pl.ds(0, user_width), cols], cross_user.at[:, cols])
        )
        item_here.append(
            copy(
                3 + count + n,
                cross_hbm.at[0, pl.ds(user_width, item_width), cols],
                cross_item.at[:, cols],
            )
        )
    slab_here.start()
    for n in range(count):
        user_here[n].start()
        item_here[n].start()
    wide[...] = msg_ref[...].astype(F32)

    def fetch(part, table, at):
        for cols in tiles(table.shape[1]):
            first[part, at + cols.start : at + cols.stop] = jnp.dot(
                items_hot[part, :], table[:, cols], preferred_element_type=F32
            ).astype(BF)

    left = iota((8, LANES), 1) < 64
    for t in range(user_width // LANES):
        for p in range(2):
            even = wide[pl.ds(8 * t + 1 + p, 8, stride=WORDS * per_req), :]
            odd = wide[pl.ds(8 * t + 5 + p, 8, stride=WORDS * per_req), :]
            users[t, pl.ds(2 * p, 8, stride=4), :] = jnp.where(left, even, pltpu.roll(odd, 64, 1))
            users[t, pl.ds(2 * p + 1, 8, stride=4), :] = jnp.where(
                left, pltpu.roll(even, 64, 1), odd
            )
    value = wide[pl.ds(0, devices, stride=WORDS), :]
    value = value * 16.0 + pltpu.roll(value, LANES - CAP, 1)
    value = value.astype(jnp.int32) - 1
    row_of = value >> 2
    req_of = (value & 3) + (iota((devices, LANES), 0) // per_req & 1) * 4
    row_lane = iota((devices, rows), 1)
    for part in parts:
        for k in range(part.start // devices, part.stop // devices):
            here = slice(k * devices, (k + 1) * devices)
            items_hot[here, :] = (row_lane == row_of[:, k : k + 1]).astype(BF)
            request[here, :] = jnp.broadcast_to(req_of[:, k : k + 1], (devices, LANES))
        fetch(part, slab_ref, user_width)
    slab_here.wait()
    for part in parts:
        fetch(part, slab_rest, user_width + staged)
    users_bf = jnp.concatenate(
        [users[t].astype(BF) for t in range(user_width // LANES)], axis=1
    )
    along_rows = lax.GatherDimensionNumbers(
        offset_dims=(),
        collapsed_slice_dims=(0,),
        start_index_map=(0,),
        operand_batching_dims=(1,),
        start_indices_batching_dims=(1,),
    )

    def of_request(rows, places):
        got = [
            lax.gather(
                rows,
                place,
                along_rows,
                slice_sizes=(1, 1),
                mode=lax.GatherScatterMode.PROMISE_IN_BOUNDS,
            )
            for place in places
        ]
        return jnp.concatenate(got, axis=0)

    def request_term(places):
        for n in places:
            user_here[n].wait()
            item_here[n].wait()
        for n in places:
            cols = columns[n]
            base = jnp.dot(users_bf, cross_user[:, cols], preferred_element_type=F32)
            shift[:, cols] = base + (cross_bias_ref[0:1, cols] + 1.0)

    def layer_one(part, cols):
        mixed = jnp.dot(first[part, user_width:], cross_item[:, cols], preferred_element_type=F32)
        for start in range(cols.start, cols.stop, LANES):
            lanes = slice(start, start + LANES)
            for at in range(part.start, part.stop, per_req):
                here = slice(at, at + per_req)
                pair = at % devices // per_req // 2 * 8
                places = [request[n : n + 8, :][:, :, None] for n in (at, at + 8)]
                factor = mixed[
                    at - part.start : at - part.start + per_req,
                    start - cols.start : start - cols.start + LANES,
                ]
                factor = factor + of_request(shift[pair : pair + 8, lanes], places)
                if start < user_width:
                    own = of_request(users[start // LANES, pair : pair + 8, :], places)
                    first[here, lanes] = own.astype(BF)
                else:
                    own = first[here, lanes].astype(F32)
                new = own * factor
                state[here, lanes] = new
                state_one[here, lanes] = new.astype(BF)

    request_term([0])
    for n, cols in enumerate(columns):
        layer_one(parts[0], cols)
        if n == 0:
            cross_two_here.start()
            hidden_here.start()
            request_term(range(1, count))
        if n == count - 1:
            cross_two_here.wait()
        layer_one(parts[1], cols)
    for part in parts:
        if part.start > 0:
            hidden_here.wait()
        for cols in tiles(cross, 2 * tile):
            mixed = jnp.dot(state_one[part, :], cross_two[:, cols], preferred_element_type=F32)
            mixed += cross_bias_ref[1:2, cols]
            new = first[part, cols].astype(F32) * mixed + state[part, cols]
            state_two[part, cols] = new.astype(BF)
    lane = iota((devices, LANES), 1)
    total = jnp.zeros((devices, LANES), F32)
    for part in range(2):
        gathered = jnp.zeros((half, LANES), F32)
        sizes = [tile] * (hid // tile)
        if part == 1:
            sizes = sizes[:-1] + [tile // 2] * 2
        start = 0
        for size in sizes:
            cols = slice(start, start + size)
            hidden = jnp.dot(
                state_two[part * half : (part + 1) * half, :],
                hidden_ref[:, cols],
                preferred_element_type=F32,
            )
            for j in range(size // LANES):
                at = start // LANES + j
                unit = hidden[:, j * LANES : (j + 1) * LANES] + hidden_bias_ref[at : at + 1, :]
                unit = jnp.maximum(unit, 0.0).astype(BF).astype(F32)
                gathered += unit * out_ref[at : at + 1, :].astype(F32)
            start += size
        logit = jnp.sum(gathered, axis=1, keepdims=True)
        for k in range(half_ranks):
            here = lane == part * half_ranks + k
            total = jnp.where(here, logit[k * devices : (k + 1) * devices, :], total)
    score_ref[...] = jax.nn.sigmoid(total)


def collect_kernel(scores_ref, key_ref, out_ref):
    groups, width = key_ref.shape
    devices = scores_ref.shape[0]
    scores = scores_ref[...]
    of_rank = [jnp.broadcast_to(scores[:, k : k + 1], (devices, width)) for k in range(CAP)]
    device = iota((devices, width), 0)
    for q in range(groups):
        key = key_ref[q : q + 1, :]
        rank = key & (CAP - 1)
        got = of_rank[0]
        for k in range(1, CAP):
            got = jnp.where(rank == k, of_rank[k], got)
        got = jnp.where(device == key >> 3, got, 0.0)
        out_ref[q : q + 1, :] = jnp.sum(got, axis=0, keepdims=True)


def per_device(
    cand_ids,
    table_slab,
    user_rows,
    cross_weight,
    cross_bias,
    hidden_weight,
    hidden_bias,
    out_weight,
):
    devices = lax.axis_size("req") * lax.axis_size("score")
    groups, width = cand_ids.shape
    slots = devices * CAP
    cross = cross_weight.shape[1]
    hid = hidden_weight.shape[1]
    vmem = pl.BlockSpec(memory_space=pltpu.VMEM)
    hbm = pl.BlockSpec(memory_space=pl.ANY)
    item_width = table_slab.shape[1]
    user_width = cross - item_width
    in_vmem = pltpu.with_memory_space_constraint
    staged = item_width // 2
    msg, key, slab = pl.pallas_call(
        prepare_kernel,
        out_shape=(
            jax.ShapeDtypeStruct((devices * WORDS, LANES), BF),
            jax.ShapeDtypeStruct((groups, width), jnp.int32),
            pltpu.VMEM((table_slab.shape[0], staged), BF),
        ),
        in_specs=[hbm, hbm, hbm],
        out_specs=(vmem, vmem, vmem),
        scratch_shapes=[
            pltpu.VMEM(cand_ids.shape, jnp.int32),
            pltpu.VMEM(user_rows.shape, BF),
            pltpu.VMEM((devices * WORDS, LANES), F32),
            pltpu.SemaphoreType.DMA((3,)),
        ],
        compiler_params=pltpu.CompilerParams(vmem_limit_bytes=16 * 2**20),
        name="prepare",
    )(in_hbm(cand_ids), in_hbm(user_rows), in_hbm(table_slab))
    asked = lax.all_to_all(msg, AXES, split_axis=0, concat_axis=0, tiled=True)
    scores = pl.pallas_call(
        score_kernel,
        out_shape=pltpu.VMEM((devices, LANES), F32),
        in_specs=[vmem, vmem, hbm, hbm, vmem, hbm, vmem, vmem],
        out_specs=vmem,
        scratch_shapes=[
            pltpu.VMEM((table_slab.shape[0], item_width - staged), BF),
            pltpu.VMEM((user_width, cross), BF),
            pltpu.VMEM((item_width, cross), BF),
            pltpu.VMEM((cross, cross), BF),
            pltpu.VMEM((cross, hid), BF),
            pltpu.SemaphoreType.DMA((11,)),
            pltpu.VMEM((devices * WORDS, LANES), F32),
            pltpu.VMEM((user_width // LANES, 32, LANES), F32),
            pltpu.VMEM((32, cross), F32),
            pltpu.VMEM((slots, LANES), jnp.int32),
            pltpu.VMEM((slots, table_slab.shape[0]), BF),
            pltpu.VMEM((slots, cross), BF),
            pltpu.VMEM((slots, cross), F32),
            pltpu.VMEM((slots, cross), BF),
            pltpu.VMEM((slots, cross), BF),
        ],
        compiler_params=pltpu.CompilerParams(vmem_limit_bytes=50 * 2**20),
        name="score",
    )(
        asked,
        in_vmem(slab, pltpu.VMEM),
        in_hbm(table_slab),
        in_hbm(cross_weight),
        in_hbm(cross_bias),
        in_hbm(hidden_weight),
        in_hbm(hidden_bias.reshape(hid // LANES, LANES)),
        in_hbm(out_weight.reshape(hid // LANES, LANES)),
    )
    answered = lax.all_to_all(scores, AXES, split_axis=0, concat_axis=0, tiled=True)
    return pl.pallas_call(
        collect_kernel,
        out_shape=jax.ShapeDtypeStruct((groups, width), F32),
        in_specs=[vmem, vmem],
        out_specs=vmem,
        compiler_params=pltpu.CompilerParams(vmem_limit_bytes=2 * 2**20),
        name="collect",
    )(answered, key)


def solution(mesh):
    placed = (
        P("req", "score"),
        P(("req", "score"), None),
        P("req", "score"),
        P(),
        P(),
        P(),
        P(),
        P(),
    )
    return jax.shard_map(
        per_device, mesh=mesh, in_specs=placed, out_specs=P("req", "score"), check_vma=False
    )
```

```python
import jax
import jax.numpy as jnp
from jax import lax
from jax.experimental import pallas as pl
from jax.experimental.pallas import tpu as pltpu
from jax.sharding import PartitionSpec as P

BF = jnp.bfloat16
F32 = jnp.float32
AXES = ("req", "score")
CAP = 8
LANES = 128
WORDS = 4


def iota(shape, axis):
    return lax.broadcasted_iota(jnp.int32, shape, axis)


def in_hbm(array):
    return pltpu.with_memory_space_constraint(array, pltpu.HBM)


def prepare_kernel(
    ids_hbm,
    user_hbm,
    slab_hbm,
    msg_ref,
    key_ref,
    slab_ref,
    ids_ref,
    user_ref,
    wide,
    copied,
):
    ids_here = pltpu.make_async_copy(ids_hbm, ids_ref, copied.at[0])
    user_here = pltpu.make_async_copy(user_hbm, user_ref, copied.at[1])
    slab_here = pltpu.make_async_copy(
        slab_hbm.at[:, pl.ds(0, slab_ref.shape[1])], slab_ref, copied.at[2]
    )
    ids_here.start()
    user_here.start()
    slab_here.start()
    ids_here.wait()
    groups, width = ids_ref.shape
    devices = msg_ref.shape[0] // WORDS
    ids = ids_ref[...]
    owner = ids >> 10
    local = ids & 1023
    upto = (iota((width, width), 0) <= iota((width, width), 1)).astype(BF)
    device_row = iota((devices, width), 0)
    base = jnp.zeros((devices, 1), F32)
    slot_values = jnp.zeros((devices, LANES), F32)
    contract_last = (((1,), (1,)), ((), ()))
    for q in range(groups):
        mine = device_row == owner[q : q + 1, :]
        onehot = mine.astype(BF)
        count = jnp.dot(onehot, upto, preferred_element_type=F32) + base
        rank = jnp.sum(jnp.where(mine, count, 0.0), axis=0, keepdims=True) - 1.0
        rank = rank.astype(jnp.int32)
        base = count[:, width - 1 : width]
        value = local[q : q + 1, :] * groups + (q + 1)
        place = iota((LANES, width), 0)
        digit = jnp.where(place == rank, value >> 4, 0)
        digit = jnp.where(place == rank + CAP, value & 15, digit)
        slot_values += lax.dot_general(
            onehot, digit.astype(F32).astype(BF), contract_last, preferred_element_type=F32
        )
        key_ref[q : q + 1, :] = owner[q : q + 1, :] * CAP + rank
    user_here.wait()
    user = user_ref[...].astype(F32)
    pairs = [
        jnp.concatenate([user[2 * p : 2 * p + 1, :], user[2 * p + 1 : 2 * p + 2, :]], axis=1)
        for p in range(2)
    ]
    wide[pl.ds(0, devices, stride=WORDS), :] = slot_values
    for p in range(2):
        wide[pl.ds(p + 1, devices, stride=WORDS), :] = jnp.broadcast_to(pairs[p], (devices, LANES))
    wide[pl.ds(3, devices, stride=WORDS), :] = jnp.zeros((devices, LANES), F32)
    msg_ref[...] = wide[...].astype(BF)
    slab_here.wait()


def score_kernel(
    msg_ref,
    slab_ref,
    slab_hbm,
    cross_hbm,
    cross_bias_ref,
    hidden_hbm,
    hidden_bias_ref,
    out_ref,
    score_ref,
    slab_rest,
    cross_user,
    cross_item,
    cross_two,
    hidden_ref,
    copied,
    wide,
    users,
    shift,
    request,
    items_hot,
    first,
    state,
    state_one,
    state_two,
):
    devices = msg_ref.shape[0] // WORDS
    rows = slab_ref.shape[0]
    staged = slab_ref.shape[1]
    item_width = staged + slab_rest.shape[1]
    cross = cross_item.shape[1]
    user_width = cross - item_width
    hid = hidden_ref.shape[1]
    slots = CAP * devices
    per_req = devices // 8
    half = slots // 2
    half_ranks = CAP // 2
    tile = 512
    parts = [slice(h, h + half) for h in range(0, slots, half)]

    def tiles(width):
        return [slice(n, n + tile) for n in range(0, width, tile)]

    def copy(i, source, target):
        return pltpu.make_async_copy(source, target, copied.at[i])

    columns = tiles(cross)
    count = len(columns)
    slab_here = copy(0, slab_hbm.at[:, pl.ds(staged, item_width - staged)], slab_rest)
    cross_two_here = copy(1, cross_hbm.at[1], cross_two)
    hidden_here = copy(2, hidden_hbm, hidden_ref)
    user_here, item_here = [], []
    for n, cols in enumerate(columns):
        cols = pl.ds(cols.start, tile)
        user_here.append(
            copy(3 + n, cross_hbm.at[0, pl.ds(0, user_width), cols], cross_user.at[:, cols])
        )
        item_here.append(
            copy(
                3 + count + n,
                cross_hbm.at[0, pl.ds(user_width, item_width), cols],
                cross_item.at[:, cols],
            )
        )
    slab_here.start()
    for n in range(count):
        user_here[n].start()
        item_here[n].start()
    wide[...] = msg_ref[...].astype(F32)

    def fetch(part, table, at):
        for cols in tiles(table.shape[1]):
            first[part, at + cols.start : at + cols.stop] = jnp.dot(
                items_hot[part, :], table[:, cols], preferred_element_type=F32
            ).astype(BF)

    value = wide[pl.ds(0, devices, stride=WORDS), :]
    value = value * 16.0 + pltpu.roll(value, LANES - CAP, 1)
    value = value.astype(jnp.int32) - 1
    row_of = value >> 2
    req_of = (value & 3) + (iota((devices, LANES), 0) // per_req & 1) * 4
    row_lane = iota((devices, rows), 1)
    for part in parts:
        for k in range(part.start // devices, part.stop // devices):
            here = slice(k * devices, (k + 1) * devices)
            items_hot[here, :] = (row_lane == row_of[:, k : k + 1]).astype(BF)
            request[here, :] = jnp.broadcast_to(req_of[:, k : k + 1], (devices, LANES))
        fetch(part, slab_ref, user_width)
    left = iota((8, LANES), 1) < 64
    for t in range(user_width // LANES):
        for p in range(2):
            even = wide[pl.ds(8 * t + 1 + p, 8, stride=WORDS * per_req), :]
            odd = wide[pl.ds(8 * t + 5 + p, 8, stride=WORDS * per_req), :]
            users[t, pl.ds(2 * p, 8, stride=4), :] = jnp.where(left, even, pltpu.roll(odd, 64, 1))
            users[t, pl.ds(2 * p + 1, 8, stride=4), :] = jnp.where(
                left, pltpu.roll(even, 64, 1), odd
            )
    slab_here.wait()
    for part in parts:
        fetch(part, slab_rest, user_width + staged)
    users_bf = jnp.concatenate(
        [users[t].astype(BF) for t in range(user_width // LANES)], axis=1
    )
    along_rows = lax.GatherDimensionNumbers(
        offset_dims=(),
        collapsed_slice_dims=(0,),
        start_index_map=(0,),
        operand_batching_dims=(1,),
        start_indices_batching_dims=(1,),
    )

    def of_request(rows, places):
        got = [
            lax.gather(
                rows,
                place,
                along_rows,
                slice_sizes=(1, 1),
                mode=lax.GatherScatterMode.PROMISE_IN_BOUNDS,
            )
            for place in places
        ]
        return jnp.concatenate(got, axis=0)

    def request_term(places):
        for n in places:
            user_here[n].wait()
            item_here[n].wait()
        for n in places:
            cols = columns[n]
            base = jnp.dot(users_bf, cross_user[:, cols], preferred_element_type=F32)
            shift[:, cols] = base + (cross_bias_ref[0:1, cols] + 1.0)

    def layer_one(part, cols):
        mixed = jnp.dot(first[part, user_width:], cross_item[:, cols], preferred_element_type=F32)
        for start in range(cols.start, cols.stop, LANES):
            lanes = slice(start, start + LANES)
            for at in range(part.start, part.stop, per_req):
                here = slice(at, at + per_req)
                pair = at % devices // per_req // 2 * 8
                places = [request[n : n + 8, :][:, :, None] for n in (at, at + 8)]
                factor = mixed[
                    at - part.start : at - part.start + per_req,
                    start - cols.start : start - cols.start + LANES,
                ]
                factor = factor + of_request(shift[pair : pair + 8, lanes], places)
                if start < user_width:
                    own = of_request(users[start // LANES, pair : pair + 8, :], places)
                    first[here, lanes] = own.astype(BF)
                else:
                    own = first[here, lanes].astype(F32)
                new = own * factor
                state[here, lanes] = new
                state_one[here, lanes] = new.astype(BF)

    request_term([0])
    for n, cols in enumerate(columns):
        layer_one(parts[0], cols)
        if n == 0:
            cross_two_here.start()
            hidden_here.start()
            request_term(range(1, count))
        if n == count - 1:
            cross_two_here.wait()
        layer_one(parts[1], cols)
    for part in parts:
        if part.start > 0:
            hidden_here.wait()
        for cols in tiles(cross):
            mixed = jnp.dot(state_one[part, :], cross_two[:, cols], preferred_element_type=F32)
            mixed += cross_bias_ref[1:2, cols]
            new = first[part, cols].astype(F32) * mixed + state[part, cols]
            state_two[part, cols] = new.astype(BF)
    lane = iota((devices, LANES), 1)
    total = jnp.zeros((devices, LANES), F32)
    for part in range(2):
        gathered = jnp.zeros((half, LANES), F32)
        for start in range(0, hid, tile):
            cols = slice(start, start + tile)
            hidden = jnp.dot(
                state_two[part * half : (part + 1) * half, :],
                hidden_ref[:, cols],
                preferred_element_type=F32,
            )
            for j in range(tile // LANES):
                at = start // LANES + j
                unit = hidden[:, j * LANES : (j + 1) * LANES] + hidden_bias_ref[at : at + 1, :]
                unit = jnp.maximum(unit, 0.0).astype(BF).astype(F32)
                gathered += unit * out_ref[at : at + 1, :].astype(F32)
        logit = jnp.sum(gathered, axis=1, keepdims=True)
        for k in range(half_ranks):
            here = lane == part * half_ranks + k
            total = jnp.where(here, logit[k * devices : (k + 1) * devices, :], total)
    score_ref[...] = jax.nn.sigmoid(total)


def collect_kernel(scores_ref, key_ref, out_ref):
    groups, width = key_ref.shape
    devices = scores_ref.shape[0]
    scores = scores_ref[...]
    of_rank = [jnp.broadcast_to(scores[:, k : k + 1], (devices, width)) for k in range(CAP)]
    device = iota((devices, width), 0)
    for q in range(groups):
        key = key_ref[q : q + 1, :]
        rank = key & (CAP - 1)
        got = of_rank[0]
        for k in range(1, CAP):
            got = jnp.where(rank == k, of_rank[k], got)
        got = jnp.where(device == key >> 3, got, 0.0)
        out_ref[q : q + 1, :] = jnp.sum(got, axis=0, keepdims=True)


def per_device(
    cand_ids,
    table_slab,
    user_rows,
    cross_weight,
    cross_bias,
    hidden_weight,
    hidden_bias,
    out_weight,
):
    devices = lax.axis_size("req") * lax.axis_size("score")
    groups, width = cand_ids.shape
    slots = devices * CAP
    cross = cross_weight.shape[1]
    hid = hidden_weight.shape[1]
    vmem = pl.BlockSpec(memory_space=pltpu.VMEM)
    hbm = pl.BlockSpec(memory_space=pl.ANY)
    item_width = table_slab.shape[1]
    user_width = cross - item_width
    in_vmem = pltpu.with_memory_space_constraint
    staged = item_width // 2
    msg, key, slab = pl.pallas_call(
        prepare_kernel,
        out_shape=(
            jax.ShapeDtypeStruct((devices * WORDS, LANES), BF),
            jax.ShapeDtypeStruct((groups, width), jnp.int32),
            pltpu.VMEM((table_slab.shape[0], staged), BF),
        ),
        in_specs=[hbm, hbm, hbm],
        out_specs=(vmem, vmem, vmem),
        scratch_shapes=[
            pltpu.VMEM(cand_ids.shape, jnp.int32),
            pltpu.VMEM(user_rows.shape, BF),
            pltpu.VMEM((devices * WORDS, LANES), F32),
            pltpu.SemaphoreType.DMA((3,)),
        ],
        compiler_params=pltpu.CompilerParams(vmem_limit_bytes=16 * 2**20),
        name="prepare",
    )(in_hbm(cand_ids), in_hbm(user_rows), in_hbm(table_slab))
    asked = lax.all_to_all(msg, AXES, split_axis=0, concat_axis=0, tiled=True)
    scores = pl.pallas_call(
        score_kernel,
        out_shape=pltpu.VMEM((devices, LANES), F32),
        in_specs=[vmem, vmem, hbm, hbm, vmem, hbm, vmem, vmem],
        out_specs=vmem,
        scratch_shapes=[
            pltpu.VMEM((table_slab.shape[0], item_width - staged), BF),
            pltpu.VMEM((user_width, cross), BF),
            pltpu.VMEM((item_width, cross), BF),
            pltpu.VMEM((cross, cross), BF),
            pltpu.VMEM((cross, hid), BF),
            pltpu.SemaphoreType.DMA((11,)),
            pltpu.VMEM((devices * WORDS, LANES), F32),
            pltpu.VMEM((user_width // LANES, 32, LANES), F32),
            pltpu.VMEM((32, cross), F32),
            pltpu.VMEM((slots, LANES), jnp.int32),
            pltpu.VMEM((slots, table_slab.shape[0]), BF),
            pltpu.VMEM((slots, cross), BF),
            pltpu.VMEM((slots, cross), F32),
            pltpu.VMEM((slots, cross), BF),
            pltpu.VMEM((slots, cross), BF),
        ],
        compiler_params=pltpu.CompilerParams(vmem_limit_bytes=50 * 2**20),
        name="score",
    )(
        asked,
        in_vmem(slab, pltpu.VMEM),
        in_hbm(table_slab),
        in_hbm(cross_weight),
        in_hbm(cross_bias),
        in_hbm(hidden_weight),
        in_hbm(hidden_bias.reshape(hid // LANES, LANES)),
        in_hbm(out_weight.reshape(hid // LANES, LANES)),
    )
    answered = lax.all_to_all(scores, AXES, split_axis=0, concat_axis=0, tiled=True)
    return pl.pallas_call(
        collect_kernel,
        out_shape=jax.ShapeDtypeStruct((groups, width), F32),
        in_specs=[vmem, vmem],
        out_specs=vmem,
        compiler_params=pltpu.CompilerParams(vmem_limit_bytes=2 * 2**20),
        name="collect",
    )(answered, key)


def solution(mesh):
    placed = (
        P("req", "score"),
        P(("req", "score"), None),
        P("req", "score"),
        P(),
        P(),
        P(),
        P(),
        P(),
    )
    return jax.shard_map(
        per_device, mesh=mesh, in_specs=placed, out_specs=P("req", "score"), check_vma=False
    )
```

```python
import jax
import jax.numpy as jnp
from jax import lax
from jax.experimental import pallas as pl
from jax.experimental.pallas import tpu as pltpu
from jax.sharding import PartitionSpec as P

BF = jnp.bfloat16
F32 = jnp.float32
AXES = ("req", "score")
CAP = 8
LANES = 128
WORDS = 4


def iota(shape, axis):
    return lax.broadcasted_iota(jnp.int32, shape, axis)


def in_hbm(array):
    return pltpu.with_memory_space_constraint(array, pltpu.HBM)


def prepare_kernel(
    ids_hbm,
    user_hbm,
    slab_hbm,
    msg_ref,
    key_ref,
    slab_ref,
    ids_ref,
    user_ref,
    wide,
    copied,
):
    ids_here = pltpu.make_async_copy(ids_hbm, ids_ref, copied.at[0])
    user_here = pltpu.make_async_copy(user_hbm, user_ref, copied.at[1])
    slab_here = pltpu.make_async_copy(
        slab_hbm.at[:, pl.ds(0, slab_ref.shape[1])], slab_ref, copied.at[2]
    )
    ids_here.start()
    user_here.start()
    slab_here.start()
    ids_here.wait()
    groups, width = ids_ref.shape
    devices = msg_ref.shape[0] // WORDS
    ids = ids_ref[...]
    owner = ids >> 10
    local = ids & 1023
    upto = (iota((width, width), 0) <= iota((width, width), 1)).astype(BF)
    device_row = iota((devices, width), 0)
    base = jnp.zeros((devices, 1), F32)
    slot_values = jnp.zeros((devices, LANES), F32)
    contract_last = (((1,), (1,)), ((), ()))
    for q in range(groups):
        mine = device_row == owner[q : q + 1, :]
        onehot = mine.astype(BF)
        count = jnp.dot(onehot, upto, preferred_element_type=F32) + base
        rank = jnp.sum(jnp.where(mine, count, 0.0), axis=0, keepdims=True) - 1.0
        rank = rank.astype(jnp.int32)
        base = count[:, width - 1 : width]
        value = local[q : q + 1, :] * groups + (q + 1)
        place = iota((LANES, width), 0)
        digit = jnp.where(place == rank, value >> 4, 0)
        digit = jnp.where(place == rank + CAP, value & 15, digit)
        slot_values += lax.dot_general(
            onehot, digit.astype(F32).astype(BF), contract_last, preferred_element_type=F32
        )
        key_ref[q : q + 1, :] = owner[q : q + 1, :] * CAP + rank
    user_here.wait()
    user = user_ref[...].astype(F32)
    pairs = [
        jnp.concatenate([user[2 * p : 2 * p + 1, :], user[2 * p + 1 : 2 * p + 2, :]], axis=1)
        for p in range(2)
    ]
    wide[pl.ds(0, devices, stride=WORDS), :] = slot_values
    for p in range(2):
        wide[pl.ds(p + 1, devices, stride=WORDS), :] = jnp.broadcast_to(pairs[p], (devices, LANES))
    wide[pl.ds(3, devices, stride=WORDS), :] = jnp.zeros((devices, LANES), F32)
    msg_ref[...] = wide[: msg_ref.shape[0], :].astype(BF)
    slab_here.wait()


def score_kernel(
    msg_ref,
    slab_ref,
    slab_hbm,
    cross_hbm,
    cross_bias_ref,
    hidden_hbm,
    hidden_bias_ref,
    out_ref,
    score_ref,
    slab_rest,
    cross_user,
    cross_item,
    cross_two,
    hidden_ref,
    copied,
    wide,
    users,
    shift,
    request,
    items_hot,
    first,
    state,
    state_one,
    state_two,
):
    devices = msg_ref.shape[0] // WORDS
    rows = slab_ref.shape[0]
    staged = slab_ref.shape[1]
    item_width = staged + slab_rest.shape[1]
    cross = cross_item.shape[1]
    user_width = cross - item_width
    hid = hidden_ref.shape[1]
    slots = CAP * devices
    per_req = devices // 8
    half = slots // 2
    half_ranks = CAP // 2
    tile = 512
    parts = [slice(h, h + half) for h in range(0, slots, half)]

    def tiles(width):
        return [slice(n, n + tile) for n in range(0, width, tile)]

    def copy(i, source, target):
        return pltpu.make_async_copy(source, target, copied.at[i])

    columns = tiles(cross)
    count = len(columns)
    slab_here = copy(0, slab_hbm.at[:, pl.ds(staged, item_width - staged)], slab_rest)
    cross_two_here = copy(1, cross_hbm.at[1], cross_two)
    hidden_here = copy(2, hidden_hbm, hidden_ref)
    user_here, item_here = [], []
    for n, cols in enumerate(columns):
        cols = pl.ds(cols.start, tile)
        user_here.append(
            copy(3 + n, cross_hbm.at[0, pl.ds(0, user_width), cols], cross_user.at[:, cols])
        )
        item_here.append(
            copy(
                3 + count + n,
                cross_hbm.at[0, pl.ds(user_width, item_width), cols],
                cross_item.at[:, cols],
            )
        )
    slab_here.start()
    for n in range(count):
        user_here[n].start()
        item_here[n].start()
    wide[: msg_ref.shape[0], :] = msg_ref[...].astype(F32)

    def fetch(part, table, at):
        for cols in tiles(table.shape[1]):
            first[part, at + cols.start : at + cols.stop] = jnp.dot(
                items_hot[part, :], table[:, cols], preferred_element_type=F32
            ).astype(BF)

    value = wide[pl.ds(0, devices, stride=WORDS), :]
    value = value * 16.0 + pltpu.roll(value, LANES - CAP, 1)
    value = value.astype(jnp.int32) - 1
    row_of = value >> 2
    req_of = (value & 3) + (iota((devices, LANES), 0) // per_req & 1) * 4
    row_lane = iota((devices, rows), 1)
    for part in parts:
        for k in range(part.start // devices, part.stop // devices):
            here = slice(k * devices, (k + 1) * devices)
            items_hot[here, :] = (row_lane == row_of[:, k : k + 1]).astype(BF)
            request[here, :] = jnp.broadcast_to(req_of[:, k : k + 1], (devices, LANES))
        fetch(part, slab_ref, user_width)
    left = iota((8, LANES), 1) < 64
    for t in range(user_width // LANES):
        for p in range(2):
            even = wide[pl.ds(8 * t + 1 + p, 8, stride=WORDS * per_req), :]
            odd = wide[pl.ds(8 * t + 5 + p, 8, stride=WORDS * per_req), :]
            users[t, pl.ds(2 * p, 8, stride=4), :] = jnp.where(left, even, pltpu.roll(odd, 64, 1))
            users[t, pl.ds(2 * p + 1, 8, stride=4), :] = jnp.where(
                left, pltpu.roll(even, 64, 1), odd
            )
    slab_here.wait()
    for part in parts:
        fetch(part, slab_rest, user_width + staged)
    users_bf = jnp.concatenate(
        [users[t, :32, :].astype(BF) for t in range(user_width // LANES)], axis=1
    )
    along_rows = lax.GatherDimensionNumbers(
        offset_dims=(),
        collapsed_slice_dims=(0,),
        start_index_map=(0,),
        operand_batching_dims=(1,),
        start_indices_batching_dims=(1,),
    )

    def of_request(rows, places):
        got = [
            lax.gather(
                rows,
                place,
                along_rows,
                slice_sizes=(1, 1),
                mode=lax.GatherScatterMode.PROMISE_IN_BOUNDS,
            )
            for place in places
        ]
        return jnp.concatenate(got, axis=0)

    def request_term(places):
        for n in places:
            user_here[n].wait()
            item_here[n].wait()
        for n in places:
            cols = columns[n]
            base = jnp.dot(users_bf, cross_user[:, cols], preferred_element_type=F32)
            shift[:, cols] = base + (cross_bias_ref[0:1, cols] + 1.0)

    def layer_one(part, cols):
        mixed = jnp.dot(first[part, user_width:], cross_item[:, cols], preferred_element_type=F32)
        for start in range(cols.start, cols.stop, LANES):
            lanes = slice(start, start + LANES)
            for at in range(part.start, part.stop, per_req):
                here = slice(at, at + per_req)
                pair = at % devices // per_req // 2 * 8
                places = [request[n : n + 8, :][:, :, None] for n in (at, at + 8)]
                factor = mixed[
                    at - part.start : at - part.start + per_req,
                    start - cols.start : start - cols.start + LANES,
                ]
                factor = factor + of_request(shift[pair : pair + 8, lanes], places)
                if start < user_width:
                    own = of_request(users[start // LANES, pair : pair + 8, :], places)
                    first[here, lanes] = own.astype(BF)
                else:
                    own = first[here, lanes].astype(F32)
                new = own * factor
                state[here, lanes] = new
                state_one[here, lanes] = new.astype(BF)

    request_term([0])
    for n, cols in enumerate(columns):
        layer_one(parts[0], cols)
        if n == 0:
            cross_two_here.start()
            hidden_here.start()
            request_term(range(1, count))
        if n == count - 1:
            cross_two_here.wait()
        layer_one(parts[1], cols)
    for part in parts:
        if part.start > 0:
            hidden_here.wait()
        for cols in tiles(cross):
            mixed = jnp.dot(state_one[part, :], cross_two[:, cols], preferred_element_type=F32)
            mixed += cross_bias_ref[1:2, cols]
            new = first[part, cols].astype(F32) * mixed + state[part, cols]
            state_two[part, cols] = new.astype(BF)
    lane = iota((devices, LANES), 1)
    total = jnp.zeros((devices, LANES), F32)
    for part in range(2):
        gathered = jnp.zeros((half, LANES), F32)
        for start in range(0, hid, tile):
            cols = slice(start, start + tile)
            hidden = jnp.dot(
                state_two[part * half : (part + 1) * half, :],
                hidden_ref[:, cols],
                preferred_element_type=F32,
            )
            for j in range(tile // LANES):
                at = start // LANES + j
                unit = hidden[:, j * LANES : (j + 1) * LANES] + hidden_bias_ref[at : at + 1, :]
                unit = jnp.maximum(unit, 0.0).astype(BF).astype(F32)
                gathered += unit * out_ref[at : at + 1, :].astype(F32)
        logit = jnp.sum(gathered, axis=1, keepdims=True)
        for k in range(half_ranks):
            here = lane == part * half_ranks + k
            total = jnp.where(here, logit[k * devices : (k + 1) * devices, :], total)
    score_ref[...] = jax.nn.sigmoid(total)


def collect_kernel(scores_ref, key_ref, out_ref):
    groups, width = key_ref.shape
    devices = scores_ref.shape[0]
    scores = scores_ref[...]
    of_rank = [jnp.broadcast_to(scores[:, k : k + 1], (devices, width)) for k in range(CAP)]
    device = iota((devices, width), 0)
    for q in range(groups):
        key = key_ref[q : q + 1, :]
        rank = key & (CAP - 1)
        got = of_rank[0]
        for k in range(1, CAP):
            got = jnp.where(rank == k, of_rank[k], got)
        got = jnp.where(device == key >> 3, got, 0.0)
        out_ref[q : q + 1, :] = jnp.sum(got, axis=0, keepdims=True)


def per_device(
    cand_ids,
    table_slab,
    user_rows,
    cross_weight,
    cross_bias,
    hidden_weight,
    hidden_bias,
    out_weight,
):
    devices = lax.axis_size("req") * lax.axis_size("score")
    groups, width = cand_ids.shape
    slots = devices * CAP
    cross = cross_weight.shape[1]
    hid = hidden_weight.shape[1]
    vmem = pl.BlockSpec(memory_space=pltpu.VMEM)
    hbm = pl.BlockSpec(memory_space=pl.ANY)
    item_width = table_slab.shape[1]
    user_width = cross - item_width
    in_vmem = pltpu.with_memory_space_constraint
    staged = item_width // 2
    msg, key, slab = pl.pallas_call(
        prepare_kernel,
        out_shape=(
            jax.ShapeDtypeStruct((devices * WORDS, LANES), BF),
            jax.ShapeDtypeStruct((groups, width), jnp.int32),
            pltpu.VMEM((table_slab.shape[0], staged), BF),
        ),
        in_specs=[hbm, hbm, hbm],
        out_specs=(vmem, vmem, vmem),
        scratch_shapes=[
            pltpu.VMEM(cand_ids.shape, jnp.int32),
            pltpu.VMEM(user_rows.shape, BF),
            pltpu.VMEM((devices * WORDS + 16 * WORDS, LANES), F32),
            pltpu.SemaphoreType.DMA((3,)),
        ],
        compiler_params=pltpu.CompilerParams(vmem_limit_bytes=16 * 2**20),
        name="prepare",
    )(in_hbm(cand_ids), in_hbm(user_rows), in_hbm(table_slab))
    asked = lax.all_to_all(msg, AXES, split_axis=0, concat_axis=0, tiled=True)
    scores = pl.pallas_call(
        score_kernel,
        out_shape=pltpu.VMEM((devices, LANES), F32),
        in_specs=[vmem, vmem, hbm, hbm, vmem, hbm, vmem, vmem],
        out_specs=vmem,
        scratch_shapes=[
            pltpu.VMEM((table_slab.shape[0], item_width - staged), BF),
            pltpu.VMEM((user_width, cross), BF),
            pltpu.VMEM((item_width, cross), BF),
            pltpu.VMEM((cross, cross), BF),
            pltpu.VMEM((cross, hid), BF),
            pltpu.SemaphoreType.DMA((11,)),
            pltpu.VMEM((devices * WORDS + 16 * WORDS, LANES), F32),
            pltpu.VMEM((user_width // LANES, 40, LANES), F32),
            pltpu.VMEM((32, cross), F32),
            pltpu.VMEM((slots, LANES), jnp.int32),
            pltpu.VMEM((slots, table_slab.shape[0]), BF),
            pltpu.VMEM((slots, cross), BF),
            pltpu.VMEM((slots, cross), F32),
            pltpu.VMEM((slots, cross), BF),
            pltpu.VMEM((slots, cross), BF),
        ],
        compiler_params=pltpu.CompilerParams(vmem_limit_bytes=50 * 2**20),
        name="score",
    )(
        asked,
        in_vmem(slab, pltpu.VMEM),
        in_hbm(table_slab),
        in_hbm(cross_weight),
        in_hbm(cross_bias),
        in_hbm(hidden_weight),
        in_hbm(hidden_bias.reshape(hid // LANES, LANES)),
        in_hbm(out_weight.reshape(hid // LANES, LANES)),
    )
    answered = lax.all_to_all(scores, AXES, split_axis=0, concat_axis=0, tiled=True)
    return pl.pallas_call(
        collect_kernel,
        out_shape=jax.ShapeDtypeStruct((groups, width), F32),
        in_specs=[vmem, vmem],
        out_specs=vmem,
        compiler_params=pltpu.CompilerParams(vmem_limit_bytes=2 * 2**20),
        name="collect",
    )(answered, key)


def solution(mesh):
    placed = (
        P("req", "score"),
        P(("req", "score"), None),
        P("req", "score"),
        P(),
        P(),
        P(),
        P(),
        P(),
    )
    return jax.shard_map(
        per_device, mesh=mesh, in_specs=placed, out_specs=P("req", "score"), check_vma=False
    )
```
